512 devices in a mesh: section: 8 (over x, core), seq: 16 (over z_hi, y), dp: 4 (over z_lo).
Axes of the slice: x: 4, y: 4, z: 16 (z_hi: 4, z_lo: 4; z = z_hi * 4 + z_lo), core: 2. Of those that a mesh axis runs over, the one named last changes fastest.
Arguments:
- frozen_queries: bfloat16 [8, 4, 2048, 4096], P('section', 'dp', 'seq'), may hold values from -128 to 128
- key_value_pairs: bfloat16 [8, 4, 2048, 1024], P('section', 'dp', 'seq'), may hold values from -8 to 8
- adapter_input: bfloat16 [8, 4, 2048, 64], P('section', 'dp', 'seq'), may hold values from -6 to 6
- adapter_up_matrix: bfloat16 [8, 64, 4096], P('section', None, 'seq'), may hold values from -0.75 to 0.75
- upstream: bfloat16 [8, 4, 2048, 4096], P('section', 'dp', 'seq'), may hold values from -6 to 6
- document_index: int32 [8, 4, 2048], P('section', 'dp'), may hold values from 0 to 15, as said below
Outputs:
- query_gradient: bfloat16 [8, 4, 2048, 4096], P('section', 'dp', 'seq')
- key_value_gradient: bfloat16 [8, 4, 2048, 1024], P('section', 'dp', 'seq')
- adapter_input_gradient: bfloat16 [8, 4, 2048, 64], P('section', 'dp', 'seq')
- adapter_up_gradient: float32 [8, 64, 4096], P('section', 'dp', 'seq')
The draws below stay inside these ranges and needn't reach their ends.
Inputs may be any that keep to these rules, and one draw needn't show every extreme that they name: `document_index`: along each pack the numbers never fall; every number appears; every document spans at most 256 positions, and one document of each pack spans exactly that many.
All inputs are finite; a program needn't handle non-finite values.
Results may differ from the reference program's by a relative error of at most 0.014.
Values may be sent and summed in bfloat16 or wider, within the bound.
A program may use at most 64 MiB of HBM per device.

```python
import math
import jax
import jax.numpy as jnp
from jax import lax

QUERY_HEADS = 32
HK = 4
HEAD_SIZE = 128
ADAPTER_RANK = 64
DOCS = 16
RELAY_SECTIONS = 8
ROLLOUT_PACKS = 4
PACK_LENGTH = 2048
GROUP = 8
QH = 2


def aligned_keys(key, tie):
    first, second, third = jax.random.split(key, 3)
    shape = (RELAY_SECTIONS, ROLLOUT_PACKS, PACK_LENGTH, HK, 2, HEAD_SIZE)
    raw_values = jax.random.normal(first, shape, jnp.float32)
    spread = jnp.exp(jax.random.uniform(second, (RELAY_SECTIONS, ROLLOUT_PACKS, PACK_LENGTH, HK, 2, 1), jnp.float32, math.log(0.5), math.log(2.0)))
    chosen = jax.random.randint(third, (RELAY_SECTIONS, ROLLOUT_PACKS, PACK_LENGTH, 1, 1, 1), 0, 48) == 0
    spread = jnp.where(chosen, 1.0, spread)
    key_value_list = raw_values * spread
    positions = jnp.arange(PACK_LENGTH).reshape(1, 1, PACK_LENGTH, 1, 1, 1)
    following = jnp.roll(key_value_list, -1, axis=2)
    following_chosen = jnp.roll(chosen, -1, axis=2) & (positions < PACK_LENGTH - 1) & (tie > 0.5)
    key_half = jnp.where(following_chosen, 0.99 * following[..., 0:1, :], key_value_list[..., 0:1, :])
    key_value_list = jnp.clip(jnp.concatenate([key_half, key_value_list[..., 1:2, :]], axis=4), -8.0, 8.0)
    return key_value_list


def draw_key_value_pairs(key, part):
    key_value_list = aligned_keys(key, 0.0)
    return key_value_list.reshape(RELAY_SECTIONS, ROLLOUT_PACKS, PACK_LENGTH, HK * 2 * HEAD_SIZE).astype(jnp.bfloat16)


def draw_frozen_queries(key, part):
    key = jax.random.fold_in(key, 11)
    first, second = jax.random.split(key, 2)
    shape = (RELAY_SECTIONS, ROLLOUT_PACKS, PACK_LENGTH, QUERY_HEADS, HEAD_SIZE)
    spread = jnp.exp(jax.random.uniform(second, (RELAY_SECTIONS, ROLLOUT_PACKS, PACK_LENGTH, QUERY_HEADS, 1), jnp.float32, math.log(0.3), math.log(3.0)))
    raw_values = jax.random.normal(first, shape, jnp.float32)
    query_values = raw_values * spread
    query_values = jnp.clip(query_values, -128.0, 128.0)
    return query_values.reshape(RELAY_SECTIONS, ROLLOUT_PACKS, PACK_LENGTH, QUERY_HEADS * HEAD_SIZE).astype(jnp.bfloat16)


def pack_documents(key):
    first, second = jax.random.split(key, 2)
    most = PACK_LENGTH // 8
    others = DOCS - 1
    extra = PACK_LENGTH - most - others
    longest = jax.random.randint(first, (), 0, DOCS).astype(jnp.int32)
    order = jax.random.permutation(second, extra + others - 1).astype(jnp.int32)
    cuts = jnp.sort(order[:others - 1])
    edges = jnp.concatenate([jnp.full((1,), -1, jnp.int32), cuts, jnp.full((1,), extra + others - 1, jnp.int32)])
    extras = (edges[1:] - edges[:-1] - 1).astype(jnp.int32)

    def settle(step, current):
        over = jnp.maximum(current - (most - 1), 0).astype(jnp.int32)
        return (current - over + jnp.roll(over, 1)).astype(jnp.int32)
    extras = lax.fori_loop(0, 4 * others, settle, extras)
    short_lengths = (extras + 1).astype(jnp.int32)
    index_list = jnp.arange(DOCS, dtype=jnp.int32)
    before = short_lengths[jnp.clip(index_list, 0, DOCS - 2)]
    after = short_lengths[jnp.clip(index_list - 1, 0, DOCS - 2)]
    lengths = jnp.where(index_list < longest, before, jnp.where(index_list == longest, most, after)).astype(jnp.int32)
    bounds = jnp.cumsum(lengths)[:-1]
    positions = jnp.arange(PACK_LENGTH, dtype=jnp.int32)
    return jnp.sum((positions[:, None] >= bounds[None, :]).astype(jnp.int32), axis=1).astype(jnp.int32)


def draw_document_index(key, part):
    key = jax.random.fold_in(key, 29)
    keys = jax.random.split(key, RELAY_SECTIONS * ROLLOUT_PACKS)
    numbers = jax.vmap(pack_documents)(keys)
    return numbers.reshape(RELAY_SECTIONS, ROLLOUT_PACKS, PACK_LENGTH).astype(jnp.int32)


def levels(key, shape, cuts, least, high):
    loudness = 1.0
    for axis_at, shards_of in cuts:
        draws = jax.random.uniform(jax.random.fold_in(jax.random.fold_in(key, 6), axis_at), (shards_of,), jnp.float32, least / len(cuts), high / len(cuts))
        loudness = loudness * jnp.repeat(jnp.exp(draws), shape[axis_at] // shards_of).reshape((-1,) + (1,) * (len(shape) - 1 - axis_at))
    return loudness


def normal_values(own_key, shape, deviation, reach, shards=(), kind=jnp.bfloat16):
    array = jax.random.normal(own_key, shape, jnp.float32) * deviation
    if len(shards) > 0:
        array = levels(own_key, shape, shards, -0.22, 0.18) * array
    return jnp.clip(array, min=-reach, max=reach).astype(kind)


def setup_inputs(seed: int = 0) -> dict:
    seeds = jax.random.split(jax.random.key(seed), 7)
    return {
        "frozen_queries": draw_frozen_queries(jax.random.fold_in(seeds[6], 71), 0),
        "key_value_pairs": draw_key_value_pairs(jax.random.fold_in(seeds[6], 71), 0),
        "adapter_input": normal_values(seeds[2], (RELAY_SECTIONS, ROLLOUT_PACKS, PACK_LENGTH, ADAPTER_RANK), 1.0, 6.0, ((0, 8), (1, 4), (2, 16))),
        "adapter_up_matrix": normal_values(seeds[3], (RELAY_SECTIONS, ADAPTER_RANK, QUERY_HEADS * HEAD_SIZE), ADAPTER_RANK ** -0.5, 0.75, ((0, 8), (2, 16))),
        "upstream": normal_values(seeds[4], (RELAY_SECTIONS, ROLLOUT_PACKS, PACK_LENGTH, QUERY_HEADS * HEAD_SIZE), 1.0, 6.0, ((0, 8), (1, 4), (2, 16))),
        "document_index": draw_document_index(jax.random.fold_in(seeds[6], 71), 0),
    }


def head_grads(query_rows, key_rows, value_rows, cotangent_rows, visible):
    scale_factor = 1.0 / math.sqrt(HEAD_SIZE)
    scores = jnp.dot(query_rows, key_rows.T, preferred_element_type=jnp.float32) * scale_factor
    scores = jnp.where(visible, scores, -jnp.inf)
    shifted = jnp.exp(scores - lax.optimization_barrier(jnp.max(scores, axis=1, keepdims=True)))
    probs = shifted / lax.optimization_barrier(jnp.sum(shifted, axis=1, keepdims=True))
    probs_low = probs.astype(jnp.bfloat16)
    dprobs = jnp.dot(cotangent_rows, value_rows.T, preferred_element_type=jnp.float32)
    deltas = lax.optimization_barrier(jnp.sum(probs * dprobs, axis=1, keepdims=True))
    dscores = (probs * (dprobs - deltas)).astype(jnp.bfloat16)
    grad_query = (jnp.dot(dscores, key_rows, preferred_element_type=jnp.float32) * scale_factor).astype(jnp.bfloat16)
    grad_key = jnp.dot(dscores.T, query_rows, preferred_element_type=jnp.float32) * scale_factor
    grad_value = jnp.dot(probs_low.T, cotangent_rows, preferred_element_type=jnp.float32)
    return (grad_query, grad_key, grad_value)

def one_sequence(item_list):
    base_query_rows, key_value_rows, adapter_input_rows, cotangent_rows, document_numbers, adapter_weight = item_list
    length = base_query_rows.shape[0]
    query_values = (base_query_rows.astype(jnp.float32) + jnp.dot(adapter_input_rows, adapter_weight, preferred_element_type=jnp.float32)).astype(jnp.bfloat16)
    positions = jnp.arange(length, dtype=jnp.int32)
    visible = (document_numbers[:, None] == document_numbers[None, :]) & (positions[:, None] >= positions[None, :])
    query_heads = query_values.reshape(length, HK, GROUP, HEAD_SIZE).transpose(1, 2, 0, 3)
    cot_heads = cotangent_rows.reshape(length, HK, GROUP, HEAD_SIZE).transpose(1, 2, 0, 3)
    pair_heads = key_value_rows.reshape(length, HK, 2, HEAD_SIZE).transpose(1, 2, 0, 3)

    def per_pair(pair_items):
        group_queries, group_pairs, group_cots = pair_items

        def per_head(head_items):
            return head_grads(head_items[0], group_pairs[0], group_pairs[1], head_items[1], visible)
        query_gradient_part, grad_k, grad_v = lax.map(per_head, (group_queries, group_cots))
        partial_sums = jnp.stack([grad_k, grad_v], axis=1).reshape(GROUP // QH, QH, 2, length, HEAD_SIZE)
        partial_sums = lax.optimization_barrier(jnp.sum(partial_sums, axis=1)).astype(jnp.bfloat16)
        partial_sums = lax.optimization_barrier(partial_sums)
        return (query_gradient_part, lax.optimization_barrier(jnp.sum(partial_sums.astype(jnp.float32), axis=0)).astype(jnp.bfloat16))
    query_gradient_part, pair_gradient_list = lax.map(per_pair, (query_heads, pair_heads, cot_heads))
    query_gradient_rows = query_gradient_part.transpose(2, 0, 1, 3).reshape(length, QUERY_HEADS * HEAD_SIZE)
    pair_gradient_rows = pair_gradient_list.transpose(2, 0, 1, 3).reshape(length, HK * 2 * HEAD_SIZE)
    adapter_input_grad_rows = jnp.dot(query_gradient_rows, adapter_weight.T, preferred_element_type=jnp.float32).astype(jnp.bfloat16)
    weight_gradient = jnp.dot(adapter_input_rows.T, query_gradient_rows, preferred_element_type=jnp.float32)
    return (query_gradient_rows, pair_gradient_rows, adapter_input_grad_rows, weight_gradient)

def reference(frozen_queries, key_value_pairs, adapter_input, adapter_up_matrix, upstream, document_index):
    incoming_value = jnp.roll(upstream, -1, axis=0)

    def single_section(section_entries):
        base_query_part, key_value_list, adapter_input_rows, cotangent_list, document_numbers, weight_matrix = section_entries

        def pack_result(pack_items):
            return one_sequence(pack_items + (weight_matrix,))
        query_gradient_part, pair_gradient_list, gradient_row_list, weight_gradient = lax.map(pack_result, (base_query_part, key_value_list, adapter_input_rows, cotangent_list, document_numbers))
        return (query_gradient_part, pair_gradient_list, gradient_row_list, lax.optimization_barrier(jnp.sum(weight_gradient, axis=0)))
    query_gradient, key_value_gradient, adapter_input_gradient, adapter_up_gradient = lax.map(single_section, (frozen_queries, key_value_pairs, adapter_input, incoming_value, document_index, adapter_up_matrix))
    return (query_gradient, key_value_gradient, adapter_input_gradient, adapter_up_gradient)
```

```python
import functools
import math

import jax
import jax.numpy as jnp
from jax import lax
from jax.experimental import pallas as pl
from jax.experimental.pallas import tpu as pltpu
from jax.sharding import PartitionSpec as P

HEAD = 128
ROWS = 128
HALF = ROWS // 2
PAIR = 2 * HEAD
WIDE = 8 * HEAD
RANK = 64
PART = RANK // 4
CHUNK = 2
SCALE = 1.0 / math.sqrt(HEAD)
LOW = -1e30
MESH = pl.DeviceIdType.MESH
BF16 = jnp.bfloat16
F32 = jnp.float32


def dot(left, right, left_dim, right_dim):
    return lax.dot_general(
        left, right, (((left_dim,), (right_dim,)), ((), ())), preferred_element_type=F32
    )


def kernel(
    q_hbm, kv_hbm, a_hbm, w_hbm, up_hbm, doc_ref,
    dq_hbm, dkv_hbm, da_ref, dw_ref,
    qf, cot, kvw, xs, wall, a_v, bias, own, dkvs, landed, ds, dso, kvo, dqv, da_acc,
    ws, wr, wz, wl, wh, wf, w_own,
    q_sem, kv_sem, a_sem, wl_sem, dq_sem, dkv_sem,
    cot_s, cot_r, az_s, az_r, ay_s, ay_r,
    n1_s, n1_r, n2_s, n2_r, fw_s, x1_s, x1_r, x2_s, x2_r,
    m1_s, m1_r, m2_s, m2_r, d1_s, d1_r, d2_s, d2_r,
    wy_s, wy_r, wl_s, wl_r, wh_s, wh_r,
):
    sec = lax.axis_index("section")
    p = lax.axis_index("seq")
    l = lax.axis_index("dp")
    y = lax.rem(p, 4)
    h = lax.div(p, 4)

    def mod4(v):
        return lax.rem(v + 8, 4)

    def at(h_, y_):
        return {"seq": h_ * 4 + y_}

    def remote(src, dst, s, r, where):
        return pltpu.make_async_remote_copy(
            src_ref=src, dst_ref=dst, send_sem=s, recv_sem=r,
            device_id=where, device_id_type=MESH,
        )

    def group(i):
        return mod4(h + i)

    def kv_cols(g):
        return pl.ds(pl.multiple_of(g * PAIR, PAIR), PAIR)

    def q_cols(g):
        return pl.ds(pl.multiple_of(g * WIDE, WIDE), WIDE)

    def load_q(i):
        return pltpu.make_async_copy(q_hbm.at[0, 0, :, q_cols(group(i))], qf.at[i], q_sem.at[i])

    def load_kv(i):
        return pltpu.make_async_copy(
            kv_hbm.at[0, 0, :, kv_cols(group(i))], kvw.at[i, pl.ds(2 * ROWS, ROWS)], kv_sem.at[i]
        )

    def load_a():
        return pltpu.make_async_copy(a_hbm.at[0, 0], a_v, a_sem)

    def load_w():
        return pltpu.make_async_copy(w_hbm.at[0], wall.at[p], wl_sem)

    def send_cot(i):
        return remote(
            up_hbm.at[0, 0, :, q_cols(group(i))], cot.at[i], cot_s.at[i], cot_r.at[i],
            {"section": lax.rem(sec + 7, 8)},
        )

    def send_az(i):
        return remote(
            w_hbm.at[0], wall.at[p], az_s.at[i - 1], az_r.at[i - 1], at(mod4(h - i), y)
        )

    def send_ay(i, d):
        shard = wall.at[group(i) * 4 + y]
        return remote(shard, shard, ay_s.at[i, d - 1], ay_r.at[i, d - 1], at(h, mod4(y + d)))

    def send_n1(i):
        return remote(
            kv_hbm.at[0, 0, :, kv_cols(group(i))], kvw.at[i, pl.ds(ROWS, ROWS)],
            n1_s.at[i], n1_r.at[i], at(h, mod4(y + 1)),
        )

    def send_n2(i):
        return remote(
            kv_hbm.at[0, 0, :, kv_cols(group(i))], kvw.at[i, pl.ds(0, ROWS)],
            n2_s.at[i], n2_r.at[i], at(h, mod4(y + 2)),
        )

    def send_fwd(i):
        return remote(
            kvw.at[i, pl.ds(ROWS, ROWS)], kvw.at[i, pl.ds(0, ROWS)],
            fw_s.at[i], n2_r.at[i], at(h, mod4(y + 1)),
        )

    def send_x1(j, first, where):
        return remote(
            kv_hbm.at[0, 0, pl.ds(first, HALF), kv_cols(group(j + 1))], xs.at[j],
            x1_s.at[j], x1_r.at[j], at(h, where),
        )

    def send_x2_own(j, first, row, src_y):
        return remote(
            kv_hbm.at[0, 0, pl.ds(first, HALF), kv_cols(group(j + 1))],
            kvw.at[j, pl.ds(row, HALF)], x2_s.at[j], x2_r.at[src_y, j], at(mod4(h + 1), 0),
        )

    def send_x2_staged(j, row, src_y):
        return remote(
            xs.at[j], kvw.at[j, pl.ds(row, HALF)], x2_s.at[j], x2_r.at[src_y, j],
            at(mod4(h + 1), 0),
        )

    def wait_x2(j, row, src_y):
        send_x2_staged(j, row, src_y).wait_recv()

    def send_m1(i):
        return remote(
            dkvs.at[i, pl.ds(ROWS, ROWS)], landed.at[i, pl.ds(0, ROWS)],
            m1_s.at[i], m1_r.at[i], at(h, mod4(y - 1)),
        )

    def send_m2(i):
        return remote(
            dkvs.at[i, pl.ds(0, ROWS)], landed.at[i, pl.ds(ROWS, ROWS)],
            m2_s.at[i], m2_r.at[i], at(h, mod4(y - 2)),
        )

    def send_d1(i, row, slot, k, where):
        return remote(
            dkvs.at[i, pl.ds(row, HALF)], ds.at[i, slot],
            d1_s.at[i, k], d1_r.at[i, slot], at(h, where),
        )

    def send_d2(i, src, row, k, where):
        return remote(
            src, landed.at[lax.rem(i + 1, 4), pl.ds(row, HALF)],
            d2_s.at[i], d2_r.at[lax.rem(i + 1, 4), k], at(mod4(h - 1), where),
        )

    def send_wy(i, d):
        to = mod4(y + d)
        return remote(ws.at[i, to], wr.at[i, d - 1], wy_s.at[i, d - 1], wy_r.at[i, d - 1], at(h, to))

    def send_wl(i, d):
        to = mod4(l + d)
        return remote(
            wz.at[i, pl.ds(pl.multiple_of(to * PART, PART), PART)], wl.at[i, d - 1],
            wl_s.at[i, d - 1], wl_r.at[i, d - 1], {"dp": to},
        )

    def send_wh(i):
        return remote(wh.at[i - 1], wf.at[i - 1], wh_s.at[i - 1], wh_r.at[i - 1], at(group(i), y))

    def store_dq(i):
        return pltpu.make_async_copy(dqv.at[i], dq_hbm.at[0, 0, :, q_cols(group(i))], dq_sem.at[i])

    def store_dkv(i):
        return pltpu.make_async_copy(
            kvo.at[i], dkv_hbm.at[0, 0, :, kv_cols(group(i))], dkv_sem.at[i]
        )

    low_h = h < 3
    high_h = h > 0

    load_w().start()
    load_a().start()
    for i in range(4):
        load_kv(i).start()
        load_q(i).start()

    bar = pltpu.get_barrier_semaphore()

    def greet(where):
        pl.semaphore_signal(bar, inc=1, device_id=where, device_id_type=MESH)

    greet({"section": lax.rem(sec + 7, 8)})
    greet({"section": lax.rem(sec + 1, 8)})
    for d in range(1, 4):
        greet(at(h, mod4(y + d)))
        greet(at(mod4(h + d), y))
        greet({"dp": mod4(l + d)})

    @pl.when((y == 0) & high_h)
    def _():
        for k in range(1, 4):
            greet(at(h - 1, k))

    @pl.when((y >= 1) & low_h)
    def _():
        greet(at(h + 1, 0))

    @pl.when((y == 1) & high_h)
    def _():
        greet(at(h - 1, 2))

    @pl.when((y == 2) & low_h)
    def _():
        greet(at(h + 1, 1))

    def docs(block):
        return doc_ref[0, :, pl.ds(pl.multiple_of(block * ROWS, ROWS), ROWS)].astype(F32)

    mine = jnp.broadcast_to(docs(p), (ROWS, ROWS))
    key_row = lax.broadcasted_iota(jnp.int32, (ROWS, ROWS), 0)
    query_col = lax.broadcasted_iota(jnp.int32, (ROWS, ROWS), 1)
    for k in range(3):
        back = 2 - k
        block = jnp.maximum(p - back, 0)
        theirs = jnp.broadcast_to(docs(block), (ROWS, ROWS)).T
        seen = theirs == mine
        if back == 0:
            seen = seen & (key_row <= query_col)
        else:
            seen = seen & (jnp.broadcast_to(p, (ROWS, ROWS)) >= back)
        bias[pl.ds(k * ROWS, ROWS), :] = jnp.where(seen, 0.0, LOW)

    @pl.when(p < 2)
    def _():
        kvw[:, pl.ds(0, ROWS), :] = jnp.zeros((4, ROWS, PAIR), BF16)

    @pl.when(p < 1)
    def _():
        kvw[:, pl.ds(ROWS, ROWS), :] = jnp.zeros((4, ROWS, PAIR), BF16)

    @pl.when((y == 3) | (p == 14))
    def _():
        landed[:, pl.ds(ROWS, ROWS), :] = jnp.zeros((4, ROWS, PAIR), BF16)

    @pl.when(p == 15)
    def _():
        landed[:, pl.ds(0, ROWS), :] = jnp.zeros((4, ROWS, PAIR), BF16)

    da_acc[...] = jnp.zeros((ROWS, RANK), F32)

    extra = (
        jnp.where((y == 0) & high_h, 3, 0)
        + jnp.where((y >= 1) & low_h, 1, 0)
        + jnp.where((y == 1) & high_h, 1, 0)
        + jnp.where((y == 2) & low_h, 1, 0)
    )
    pl.semaphore_wait(bar, 11 + extra)

    @pl.when((y == 2) & low_h)
    def _():
        for j in range(4):
            send_x1(j, HALF, 1).start()
        for j in range(4):
            send_x2_own(j, 0, 0, 2).start()

    @pl.when((y == 3) & low_h)
    def _():
        for j in range(4):
            send_x1(j, 0, 0).start()
        for j in range(4):
            send_x2_own(j, HALF, 192, 3).start()

    load_w().wait()
    for d in (1, 3, 2):
        send_ay(0, d).start()
    send_cot(0).start()
    for i in (1, 3, 2):
        send_az(i).start()

    for i in range(4):
        @pl.when(y < 3)
        def _():
            send_n1(i).start()

        @pl.when(y < 2)
        def _():
            send_n2(i).start()

    for i in range(1, 4):
        send_cot(i).start()

    @pl.when((y == 1) & low_h)
    def _():
        for j in range(4):
            send_x1(j, HALF, 1).wait_recv()
            send_x2_staged(j, 64, 1).start()

    @pl.when((y == 0) & low_h)
    def _():
        for j in range(4):
            send_x1(j, 0, 0).wait_recv()
            send_x2_staged(j, 128, 0).start()

    for i in (1, 3, 2):
        send_az(i).wait_recv()
        for d in (1, 3, 2):
            send_ay(i, d).start()

    load_a().wait()

    def work(i):
        g = group(i)
        for d in (1, 3, 2):
            send_ay(i, d).wait_recv()
        load_q(i).wait()
        load_kv(i).wait()

        @pl.when(y >= 1)
        def _():
            send_n1(i).wait_recv()

        @pl.when((y >= 2) | ((y == 1) & high_h))
        def _():
            send_n2(i).wait_recv()

        @pl.when((y == 0) & high_h)
        def _():
            wait_x2(i, 128, 0)
            wait_x2(i, 192, 3)
            send_fwd(i).start()
            wait_x2(i, 64, 1)
            wait_x2(i, 0, 2)

        send_cot(i).wait_recv()

        a_rows = a_v[...]
        w_g = jnp.concatenate([wall[g * 4 + k] for k in range(4)], axis=1)
        keys = kvw[i, :, :HEAD]
        values = kvw[i, :, HEAD:]
        d_key = jnp.zeros((3 * ROWS, HEAD), F32)
        d_value = jnp.zeros((3 * ROWS, HEAD), F32)
        da = da_acc[...]
        seen = bias[...]
        seen = jnp.concatenate([seen] * CHUNK, axis=1)
        for first in range(0, 8, CHUNK):
            cols = slice(first * HEAD, (first + CHUNK) * HEAD)
            w_cols = w_g[:, cols]
            queries = (qf[i, :, cols].astype(F32) + dot(a_rows, w_cols, 1, 0)).astype(BF16)
            cots = cot[i, :, cols]
            q_rows = jnp.concatenate(
                [queries[:, k * HEAD:(k + 1) * HEAD] for k in range(CHUNK)], axis=0
            )
            c_rows = jnp.concatenate(
                [cots[:, k * HEAD:(k + 1) * HEAD] for k in range(CHUNK)], axis=0
            )
            scores = dot(keys, q_rows, 1, 1) * (SCALE * math.log2(math.e)) + seen
            top = jnp.max(scores, axis=0, keepdims=True)
            raised = jnp.exp2(scores - top)
            probs = raised * (1.0 / jnp.sum(raised, axis=0, keepdims=True))
            dprobs = dot(values, c_rows, 1, 1)
            deltas = jnp.sum(probs * dprobs, axis=0, keepdims=True)
            dscores = (probs * (dprobs - deltas)).astype(BF16)
            d_value = d_value + dot(probs.astype(BF16), c_rows, 1, 0)
            d_key = d_key + dot(dscores, q_rows, 1, 0)
            dq_rows = (dot(dscores, keys, 0, 0) * SCALE).astype(BF16)
            dq = jnp.concatenate(
                [dq_rows[k * ROWS:(k + 1) * ROWS] for k in range(CHUNK)], axis=1
            )
            dqv[i, :, cols] = dq
            da = da + dot(dq, w_cols, 1, 1)
        da_acc[...] = da
        store_dq(i).start()
        grads = jnp.concatenate([d_key * SCALE, d_value], axis=1)
        own[i] = grads[2 * ROWS:]
        dkvs[i] = grads[:2 * ROWS].astype(BF16)

        @pl.when((y == 0) & high_h)
        def _():
            send_d1(i, 0, 0, 0, 2).start()
            send_d1(i, 64, 0, 1, 1).start()
            send_d1(i, 192, 0, 2, 3).start()

        @pl.when((y == 1) & high_h)
        def _():
            send_d1(i, 0, 0, 0, 0).start()
            send_d1(i, 64, 1, 1, 3).start()

        @pl.when(y >= 1)
        def _():
            send_m1(i).start()

        @pl.when(y >= 2)
        def _():
            send_m2(i).start()

        dw = dot(a_rows, dqv[i], 0, 0).astype(BF16)
        for k in range(4):
            ws[i, k] = dw[:, k * 256:(k + 1) * 256]
        for d in (1, 3, 2):
            send_wy(i, d).start()

    def second(i):
        @pl.when((y == 0) & high_h)
        def _():
            send_d1(i, 0, 0, 0, 0).wait_recv()
            dso[i] = (ds[i, 0].astype(F32) + dkvs[i, pl.ds(ROWS, HALF), :].astype(F32)).astype(BF16)
            send_d2(i, dso.at[i], 0, 0, 3).start()

        @pl.when((y == 3) & high_h)
        def _():
            send_d1(i, 0, 0, 0, 0).wait_recv()
            send_d1(i, 0, 1, 0, 0).wait_recv()
            dso[i] = (ds[i, 0].astype(F32) + ds[i, 1].astype(F32)).astype(BF16)
            send_d2(i, dso.at[i], 64, 1, 3).start()

        @pl.when((y == 1) & high_h)
        def _():
            send_d1(i, 0, 0, 0, 0).wait_recv()
            send_d2(i, ds.at[i, 0], 192, 1, 2).start()

        @pl.when((y == 2) & high_h)
        def _():
            send_d1(i, 0, 0, 0, 0).wait_recv()
            send_d2(i, ds.at[i, 0], 128, 0, 2).start()

        total = ws[i, y].astype(F32)
        for d in range(1, 4):
            send_wy(i, d).wait_recv()
            total = total + wr[i, d - 1].astype(F32)
        wz[i] = total.astype(BF16)
        for d in (1, 3, 2):
            send_wl(i, d).start()

    def third(i):
        total = wz[i, pl.ds(pl.multiple_of(l * PART, PART), PART), :].astype(F32)
        for d in range(1, 4):
            send_wl(i, d).wait_recv()
            total = total + wl[i, d - 1].astype(F32)

        @pl.when(i == 0)
        def _():
            w_own[...] = total

        @pl.when(i > 0)
        def _():
            wh[i - 1] = total.astype(BF16)
            send_wh(i).start()

    def round_(r, _):
        @pl.when(r < 4)
        def _():
            work(r)

        @pl.when((r >= 1) & (r < 5))
        def _():
            second(r - 1)

        @pl.when(r >= 2)
        def _():
            third(r - 2)

        return 0

    lax.fori_loop(0, 6, round_, 0)

    da_ref[0, 0] = da_acc[...].astype(BF16)

    def settle(i, _):
        @pl.when(y < 3)
        def _():
            send_m1(i).wait_recv()

        @pl.when(y < 2)
        def _():
            send_m2(i).wait_recv()

        @pl.when((y >= 2) & low_h)
        def _():
            send_d2(lax.rem(i + 3, 4), ds.at[i, 0], 0, 0, 2).wait_recv()
            send_d2(lax.rem(i + 3, 4), ds.at[i, 0], 0, 1, 2).wait_recv()

        total = (
            own[i]
            + landed[i, pl.ds(0, ROWS), :].astype(F32)
            + landed[i, pl.ds(ROWS, ROWS), :].astype(F32)
        )
        kvo[i] = total.astype(BF16)
        store_dkv(i).start()
        return 0

    lax.fori_loop(0, 4, settle, 0)
    total = w_own[...]
    for i in range(1, 4):
        send_wh(i).wait_recv()
        total = total + wf[i - 1].astype(F32)
    dw_ref[0] = total

    def drain(i, _):
        send_cot(i).wait_send()
        for d in range(1, 4):
            send_ay(i, d).wait_send()
            send_wy(i, d).wait_send()
            send_wl(i, d).wait_send()

        @pl.when(i > 0)
        def _():
            send_az(i).wait_send()
            send_wh(i).wait_send()

        @pl.when(y < 3)
        def _():
            send_n1(i).wait_send()

        @pl.when((y < 2))
        def _():
            send_n2(i).wait_send()

        @pl.when((y >= 2) & low_h)
        def _():
            send_x1(i, 0, 0).wait_send()

        @pl.when(low_h)
        def _():
            send_x2_staged(i, 0, 0).wait_send()

        @pl.when(y >= 1)
        def _():
            send_m1(i).wait_send()

        @pl.when(y >= 2)
        def _():
            send_m2(i).wait_send()

        @pl.when((y < 2) & high_h)
        def _():
            send_d1(i, 0, 0, 0, 0).wait_send()
            send_d1(i, 0, 0, 1, 0).wait_send()

        @pl.when((y == 0) & high_h)
        def _():
            send_d1(i, 0, 0, 2, 0).wait_send()
            send_fwd(i).wait_send()

        @pl.when(high_h)
        def _():
            send_d2(i, ds.at[i, 0], 0, 0, 2).wait_send()

        store_dq(i).wait()
        store_dkv(i).wait()
        return 0

    lax.fori_loop(0, 4, drain, 0)


def per_device(frozen_queries, key_value_pairs, adapter_input, adapter_up_matrix, upstream, document_index):
    any_ = pl.BlockSpec(memory_space=pl.ANY)
    vmem = pl.BlockSpec(memory_space=pltpu.VMEM)
    dma = pltpu.SemaphoreType.DMA
    scratch = [
        pltpu.VMEM((4, ROWS, WIDE), BF16),
        pltpu.VMEM((4, ROWS, WIDE), BF16),
        pltpu.VMEM((4, 3 * ROWS, PAIR), BF16),
        pltpu.VMEM((4, HALF, PAIR), BF16),
        pltpu.VMEM((16, RANK, 256), BF16),
        pltpu.VMEM((ROWS, RANK), BF16),
        pltpu.VMEM((3 * ROWS, ROWS), F32),
        pltpu.VMEM((4, ROWS, PAIR), F32),
        pltpu.VMEM((4, 2 * ROWS, PAIR), BF16),
        pltpu.VMEM((4, 2 * ROWS, PAIR), BF16),
        pltpu.VMEM((4, 2, HALF, PAIR), BF16),
        pltpu.VMEM((4, HALF, PAIR), BF16),
        pltpu.VMEM((4, ROWS, PAIR), BF16),
        pltpu.VMEM((4, ROWS, WIDE), BF16),
        pltpu.VMEM((ROWS, RANK), F32),
        pltpu.VMEM((4, 4, RANK, 256), BF16),
        pltpu.VMEM((4, 3, RANK, 256), BF16),
        pltpu.VMEM((4, RANK, 256), BF16),
        pltpu.VMEM((4, 3, PART, 256), BF16),
        pltpu.VMEM((3, PART, 256), BF16),
        pltpu.VMEM((3, PART, 256), BF16),
        pltpu.VMEM((PART, 256), F32),
        dma((4,)), dma((4,)), dma, dma, dma((4,)), dma((4,)),
        dma((4,)), dma((4,)), dma((3,)), dma((3,)), dma((4, 3)), dma((4, 3)),
        dma((4,)), dma((4,)), dma((4,)), dma((4,)), dma((4,)),
        dma((4,)), dma((4,)), dma((4,)), dma((4, 4)),
        dma((4,)), dma((4,)), dma((4,)), dma((4,)),
        dma((4, 3)), dma((4, 2)), dma((4,)), dma((4, 2)),
        dma((4, 3)), dma((4, 3)), dma((4, 3)), dma((4, 3)), dma((3,)), dma((3,)),
    ]
    return pl.pallas_call(
        kernel,
        out_shape=(
            jax.ShapeDtypeStruct((1, 1, ROWS, 4 * WIDE), BF16),
            jax.ShapeDtypeStruct((1, 1, ROWS, 4 * PAIR), BF16),
            jax.ShapeDtypeStruct((1, 1, ROWS, RANK), BF16),
            jax.ShapeDtypeStruct((1, PART, 256), F32),
        ),
        in_specs=[any_, any_, any_, any_, any_, vmem],
        out_specs=(any_, any_, vmem, vmem),
        scratch_shapes=scratch,
        compiler_params=pltpu.CompilerParams(
            collective_id=0, has_side_effects=True, vmem_limit_bytes=48 << 20
        ),
    )(frozen_queries, key_value_pairs, adapter_input, adapter_up_matrix, upstream, document_index)


def solution(mesh):
    placed = (
        P("section", "dp", "seq", None),
        P("section", "dp", "seq", None),
        P("section", "dp", "seq", None),
        P("section", None, "seq"),
        P("section", "dp", "seq", None),
        P("section", "dp", None),
    )
    return jax.shard_map(
        per_device,
        mesh=mesh,
        in_specs=placed,
        out_specs=(
            P("section", "dp", "seq", None),
            P("section", "dp", "seq", None),
            P("section", "dp", "seq", None),
            P("section", "dp", "seq"),
        ),
        check_vma=False,
    )
```

```python
import functools
import math

import jax
import jax.numpy as jnp
from jax import lax
from jax.experimental import pallas as pl
from jax.experimental.pallas import tpu as pltpu
from jax.sharding import PartitionSpec as P

HEAD = 128
ROWS = 128
HALF = ROWS // 2
PAIR = 2 * HEAD
WIDE = 8 * HEAD
RANK = 64
PART = RANK // 4
CHUNK = 8
SCALE = 1.0 / math.sqrt(HEAD)
LOW = -1e30
MESH = pl.DeviceIdType.MESH
BF16 = jnp.bfloat16
F32 = jnp.float32


def dot(left, right, left_dim, right_dim):
    return lax.dot_general(
        left, right, (((left_dim,), (right_dim,)), ((), ())), preferred_element_type=F32
    )


def kernel(
    q_hbm, kv_hbm, a_hbm, w_hbm, up_hbm, doc_ref,
    dqv, kvo, da_ref, dw_ref,
    qf, cot, kvw, xs, wall, a_v, bias, own, dkvs, landed, ds, dso, da_acc,
    ws, wr, wz, wl, wh, wf, w_own,
    q_sem, kv_sem, a_sem, wl_sem,
    cot_s, cot_r, az_s, az_r, ay_s, ay_r,
    n1_s, n1_r, n2_s, n2_r, fw_s, x1_s, x1_r, x2_s, x2_r,
    m1_s, m1_r, m2_s, m2_r, d1_s, d1_r, d2_s, d2_r,
    wy_s, wy_r, wl_s, wl_r, wh_s, wh_r,
):
    sec = lax.axis_index("section")
    p = lax.axis_index("seq")
    l = lax.axis_index("dp")
    y = lax.rem(p, 4)
    h = lax.div(p, 4)

    def mod4(v):
        return lax.rem(v + 8, 4)

    def at(h_, y_):
        return {"seq": h_ * 4 + y_}

    def remote(src, dst, s, r, where):
        return pltpu.make_async_remote_copy(
            src_ref=src, dst_ref=dst, send_sem=s, recv_sem=r,
            device_id=where, device_id_type=MESH,
        )

    def group(i, at_h=None):
        at_h = h if at_h is None else at_h
        gray = jnp.where(i < 2, i, 5 - i)
        third = jnp.where(i == 0, 0, jnp.where(i == 1, 3, i - 1))
        return jnp.where(at_h == 1, i, jnp.where(at_h == 3, third, gray))

    def kv_cols(g):
        return pl.ds(pl.multiple_of(g * PAIR, PAIR), PAIR)

    def q_cols(g):
        return pl.ds(pl.multiple_of(g * WIDE, WIDE), WIDE)

    def load_q(g):
        return pltpu.make_async_copy(q_hbm.at[0, 0, :, q_cols(g)], qf.at[g], q_sem.at[g])

    def load_kv(g):
        return pltpu.make_async_copy(
            kv_hbm.at[0, 0, :, kv_cols(g)], kvw.at[g, pl.ds(2 * ROWS, ROWS)], kv_sem.at[g]
        )

    def load_a():
        return pltpu.make_async_copy(a_hbm.at[0, 0], a_v, a_sem)

    def load_w():
        return pltpu.make_async_copy(w_hbm.at[0], wall.at[p], wl_sem)

    def send_cot(g):
        return remote(
            up_hbm.at[0, 0, :, q_cols(g)], cot.at[g], cot_s.at[g], cot_r.at[g],
            {"section": lax.rem(sec + 7, 8)},
        )

    def send_az(shard, slot, there, to):
        src = wall.at[shard * 4 + y]
        return remote(src, src, az_s.at[slot], az_r.at[there], at(to, y))

    def send_az_up():
        return send_az(h, 0, 2, mod4(h + 1))

    def send_az_down():
        return send_az(h, 1, 0, mod4(h - 1))

    def send_az_relay():
        return send_az(mod4(h + 1), 2, 1, mod4(h - 1))

    def wait_az(away):
        send_az(h, 0, away - 1, mod4(h + 1)).wait_recv()

    def send_ay(g, d):
        shard = wall.at[g * 4 + y]
        return remote(shard, shard, ay_s.at[g, d - 1], ay_r.at[g, d - 1], at(h, mod4(y + d)))

    def mine(g, first, rows):
        return kvw.at[g, pl.ds(2 * ROWS + first, rows)]

    def send_n1(g):
        return remote(
            mine(g, 0, ROWS), kvw.at[g, pl.ds(ROWS, ROWS)],
            n1_s.at[g], n1_r.at[g], at(h, mod4(y + 1)),
        )

    def send_n2(g):
        return remote(
            mine(g, 0, ROWS), kvw.at[g, pl.ds(0, ROWS)],
            n2_s.at[g], n2_r.at[g], at(h, mod4(y + 2)),
        )

    def send_fwd(g):
        return remote(
            kvw.at[g, pl.ds(ROWS, ROWS)], kvw.at[g, pl.ds(0, ROWS)],
            fw_s.at[g], n2_r.at[g], at(h, mod4(y + 1)),
        )

    def send_x1(g, first, where):
        return remote(
            mine(g, first, HALF), xs.at[g], x1_s.at[g], x1_r.at[g], at(h, where)
        )

    def send_x2_own(g, first, row, src_y):
        return remote(
            mine(g, first, HALF), kvw.at[g, pl.ds(row, HALF)],
            x2_s.at[g], x2_r.at[src_y, g], at(mod4(h + 1), 0),
        )

    def send_x2_staged(g, row, src_y):
        return remote(
            xs.at[g], kvw.at[g, pl.ds(row, HALF)], x2_s.at[g], x2_r.at[src_y, g],
            at(mod4(h + 1), 0),
        )

    def wait_x2(g, row, src_y):
        send_x2_staged(g, row, src_y).wait_recv()

    def send_m1(g):
        return remote(
            dkvs.at[g, pl.ds(ROWS, ROWS)], landed.at[g, pl.ds(0, ROWS)],
            m1_s.at[g], m1_r.at[g], at(h, mod4(y - 1)),
        )

    def send_m2(g):
        return remote(
            dkvs.at[g, pl.ds(0, ROWS)], landed.at[g, pl.ds(ROWS, ROWS)],
            m2_s.at[g], m2_r.at[g], at(h, mod4(y - 2)),
        )

    def send_d1(g, row, slot, k, where):
        return remote(
            dkvs.at[g, pl.ds(row, HALF)], ds.at[g, slot],
            d1_s.at[g, k], d1_r.at[g, slot], at(h, where),
        )

    def send_d2(g, src, row, k, where):
        return remote(
            src, landed.at[g, pl.ds(row, HALF)],
            d2_s.at[g], d2_r.at[g, k], at(mod4(h - 1), where),
        )

    def send_wy(g, d):
        to = mod4(y + d)
        return remote(ws.at[g, to], wr.at[g, d - 1], wy_s.at[g, d - 1], wy_r.at[g, d - 1], at(h, to))

    def send_wl(g, d):
        to = mod4(l + d)
        return remote(
            wz.at[g, pl.ds(pl.multiple_of(to * PART, PART), PART)], wl.at[g, d - 1],
            wl_s.at[g, d - 1], wl_r.at[g, d - 1], {"dp": to},
        )

    def send_wh(g):
        slot = mod4(h - g + 3)
        return remote(wh.at[g], wf.at[slot], wh_s.at[g], wh_r.at[slot], at(g, y))

    def wait_wh(slot):
        remote(wh.at[0], wf.at[slot], wh_s.at[0], wh_r.at[slot], at(mod4(h + 1), y)).wait_recv()

    low_h = h < 3
    high_h = h > 0

    load_w().start()
    for g in range(4):
        load_kv(g).start()
    load_a().start()
    for g in range(4):
        load_q(g).start()

    bar = pltpu.get_barrier_semaphore()

    def greet(where):
        pl.semaphore_signal(bar, inc=1, device_id=where, device_id_type=MESH)

    greet({"section": lax.rem(sec + 7, 8)})
    greet({"section": lax.rem(sec + 1, 8)})
    greet(at(mod4(h + 1), y))
    greet(at(mod4(h - 1), y))
    for d in range(1, 4):
        greet(at(h, mod4(y + d)))
        greet({"dp": mod4(l + d)})

    @pl.when((y == 0) & high_h)
    def _():
        for k in range(1, 4):
            greet(at(h - 1, k))

    @pl.when((y >= 1) & low_h)
    def _():
        greet(at(h + 1, 0))

    @pl.when((y == 1) & high_h)
    def _():
        greet(at(h - 1, 2))

    @pl.when((y == 2) & low_h)
    def _():
        greet(at(h + 1, 1))

    def docs(block):
        return doc_ref[0, :, pl.ds(pl.multiple_of(block * ROWS, ROWS), ROWS)].astype(F32)

    my_docs = jnp.broadcast_to(docs(p), (ROWS, ROWS))
    key_row = lax.broadcasted_iota(jnp.int32, (ROWS, ROWS), 0)
    query_col = lax.broadcasted_iota(jnp.int32, (ROWS, ROWS), 1)
    for k in range(3):
        back = 2 - k
        block = jnp.maximum(p - back, 0)
        theirs = jnp.broadcast_to(docs(block), (ROWS, ROWS)).T
        seen = theirs == my_docs
        if back == 0:
            seen = seen & (key_row <= query_col)
        else:
            seen = seen & (jnp.broadcast_to(p, (ROWS, ROWS)) >= back)
        bias[pl.ds(k * ROWS, ROWS), :] = jnp.where(seen, 0.0, LOW)

    @pl.when(p < 2)
    def _():
        kvw[:, pl.ds(0, ROWS), :] = jnp.zeros((4, ROWS, PAIR), BF16)

    @pl.when(p < 1)
    def _():
        kvw[:, pl.ds(ROWS, ROWS), :] = jnp.zeros((4, ROWS, PAIR), BF16)

    @pl.when((y == 3) | (p == 14))
    def _():
        landed[:, pl.ds(ROWS, ROWS), :] = jnp.zeros((4, ROWS, PAIR), BF16)

    @pl.when(p == 15)
    def _():
        landed[:, pl.ds(0, ROWS), :] = jnp.zeros((4, ROWS, PAIR), BF16)

    da_acc[...] = jnp.zeros((RANK, ROWS), F32)

    extra = (
        jnp.where((y == 0) & high_h, 3, 0)
        + jnp.where((y >= 1) & low_h, 1, 0)
        + jnp.where((y == 1) & high_h, 1, 0)
        + jnp.where((y == 2) & low_h, 1, 0)
    )
    pl.semaphore_wait(bar, 10 + extra)

    for g in range(4):
        load_kv(g).wait()

    @pl.when((y == 2) & low_h)
    def _():
        for j in range(4):
            send_x1(group(j, h + 1), HALF, 1).start()
        for j in range(4):
            send_x2_own(group(j, h + 1), 0, 0, 2).start()

    @pl.when((y == 3) & low_h)
    def _():
        for j in range(4):
            send_x1(group(j, h + 1), 0, 0).start()
        for j in range(4):
            send_x2_own(group(j, h + 1), HALF, 192, 3).start()

    load_w().wait()
    for d in (1, 3, 2):
        send_ay(h, d).start()
    send_az_down().start()
    send_cot(group(0)).start()
    send_az_up().start()

    for i in range(4):
        g = group(i)
        if i > 0:
            send_cot(g).start()

        @pl.when(y < 3)
        def _():
            send_n1(g).start()

        @pl.when(y < 2)
        def _():
            send_n2(g).start()

    @pl.when((y == 1) & low_h)
    def _():
        for j in range(4):
            g = group(j, h + 1)
            send_x1(g, HALF, 1).wait_recv()
            send_x2_staged(g, 64, 1).start()

    @pl.when((y == 0) & low_h)
    def _():
        for j in range(4):
            g = group(j, h + 1)
            send_x1(g, 0, 0).wait_recv()
            send_x2_staged(g, 128, 0).start()

    def pass_shard(g):
        away = mod4(g - h)

        @pl.when(away > 0)
        def _():
            wait_az(away)

            @pl.when(away == 1)
            def _():
                send_az_relay().start()

            for d in (1, 3, 2):
                send_ay(g, d).start()

    pass_shard(group(0))
    load_a().wait()

    def work(r):
        i = group(r)
        g = i
        load_q(i).wait()

        @pl.when((y == 0) & high_h)
        def _():
            wait_x2(i, 128, 0)
            wait_x2(i, 192, 3)
            send_fwd(i).start()
            wait_x2(i, 64, 1)
            wait_x2(i, 0, 2)

        @pl.when(y >= 1)
        def _():
            send_n1(i).wait_recv()

        @pl.when((y >= 2) | ((y == 1) & high_h))
        def _():
            send_n2(i).wait_recv()

        send_cot(i).wait_recv()

        @pl.when(r < 3)
        def _():
            pass_shard(group(jnp.minimum(r + 1, 3)))

        for d in (1, 3, 2):
            send_ay(i, d).wait_recv()

        a_cols = a_v[...]
        w_g = jnp.concatenate([wall[g * 4 + k] for k in range(4)], axis=1)
        keys = kvw[i, :, :HEAD]
        values = kvw[i, :, HEAD:]
        d_key = jnp.zeros((3 * ROWS, HEAD), F32)
        d_value = jnp.zeros((3 * ROWS, HEAD), F32)
        da = da_acc[...]
        seen = bias[...]
        seen = jnp.concatenate([seen] * CHUNK, axis=1)
        for first in range(0, 8, CHUNK):
            cols = slice(first * HEAD, (first + CHUNK) * HEAD)
            w_cols = w_g[:, cols]
            queries = (qf[i, :, cols].astype(F32) + dot(a_cols, w_cols, 0, 0)).astype(BF16)
            cots = cot[i, :, cols]
            q_rows = jnp.concatenate(
                [queries[:, k * HEAD:(k + 1) * HEAD] for k in range(CHUNK)], axis=0
            )
            c_rows = jnp.concatenate(
                [cots[:, k * HEAD:(k + 1) * HEAD] for k in range(CHUNK)], axis=0
            )
            scores = dot(keys, q_rows, 1, 1) * (SCALE * math.log2(math.e)) + seen
            top = jnp.max(scores, axis=0, keepdims=True)
            raised = jnp.exp2(scores - top)
            probs = raised * (1.0 / jnp.sum(raised, axis=0, keepdims=True))
            dprobs = dot(values, c_rows, 1, 1)
            deltas = jnp.sum(probs * dprobs, axis=0, keepdims=True)
            dscores = (probs * (dprobs - deltas)).astype(BF16)
            d_value = d_value + dot(probs.astype(BF16), c_rows, 1, 0)
            d_key = d_key + dot(dscores, q_rows, 1, 0)
            dq_rows = (dot(dscores, keys, 0, 0) * SCALE).astype(BF16)
            dq = jnp.concatenate(
                [dq_rows[k * ROWS:(k + 1) * ROWS] for k in range(CHUNK)], axis=1
            )
            dqv[i, :, cols] = dq
            da = da + dot(w_cols, dq, 1, 1)
        da_acc[...] = da
        grads = jnp.concatenate([d_key * SCALE, d_value], axis=1)
        own[i] = grads[2 * ROWS:]
        dkvs[i] = grads[:2 * ROWS].astype(BF16)

        @pl.when((y == 0) & high_h)
        def _():
            send_d1(i, 0, 0, 0, 2).start()
            send_d1(i, 64, 0, 1, 1).start()
            send_d1(i, 192, 0, 2, 3).start()

        @pl.when((y == 1) & high_h)
        def _():
            send_d1(i, 0, 0, 0, 0).start()
            send_d1(i, 64, 1, 1, 3).start()

        @pl.when(y >= 1)
        def _():
            send_m1(i).start()

        @pl.when(y >= 2)
        def _():
            send_m2(i).start()

        dw = dot(a_cols, dqv[i], 1, 0).astype(BF16)
        for k in range(4):
            ws[i, k] = dw[:, k * 256:(k + 1) * 256]
        for d in (1, 3, 2):
            send_wy(i, d).start()

    def second(r):
        i = group(r)

        @pl.when((y == 0) & high_h)
        def _():
            send_d1(i, 0, 0, 0, 0).wait_recv()
            dso[i] = (ds[i, 0].astype(F32) + dkvs[i, pl.ds(ROWS, HALF), :].astype(F32)).astype(BF16)
            send_d2(i, dso.at[i], 0, 0, 3).start()

        @pl.when((y == 3) & high_h)
        def _():
            send_d1(i, 0, 0, 0, 0).wait_recv()
            send_d1(i, 0, 1, 0, 0).wait_recv()
            dso[i] = (ds[i, 0].astype(F32) + ds[i, 1].astype(F32)).astype(BF16)
            send_d2(i, dso.at[i], 64, 1, 3).start()

        @pl.when((y == 1) & high_h)
        def _():
            send_d1(i, 0, 0, 0, 0).wait_recv()
            send_d2(i, ds.at[i, 0], 192, 1, 2).start()

        @pl.when((y == 2) & high_h)
        def _():
            send_d1(i, 0, 0, 0, 0).wait_recv()
            send_d2(i, ds.at[i, 0], 128, 0, 2).start()

        total = ws[i, y].astype(F32)
        for d in range(1, 4):
            send_wy(i, d).wait_recv()
            total = total + wr[i, d - 1].astype(F32)
        wz[i] = total.astype(BF16)
        for d in (1, 3, 2):
            send_wl(i, d).start()

    def third(r):
        i = group(r)
        total = wz[i, pl.ds(pl.multiple_of(l * PART, PART), PART), :].astype(F32)
        for d in range(1, 4):
            send_wl(i, d).wait_recv()
            total = total + wl[i, d - 1].astype(F32)

        @pl.when(i == h)
        def _():
            w_own[...] = total

        @pl.when(i != h)
        def _():
            wh[i] = total.astype(BF16)
            send_wh(i).start()

    def round_(r, _):
        @pl.when(r < 4)
        def _():
            work(r)

        @pl.when((r >= 1) & (r < 5))
        def _():
            second(r - 1)

        @pl.when(r >= 2)
        def _():
            third(r - 2)

        return 0

    lax.fori_loop(0, 6, round_, 0)

    da_ref[...] = da_acc[...].astype(BF16)

    def settle(r, _):
        g = group(r)

        @pl.when(y < 3)
        def _():
            send_m1(g).wait_recv()

        @pl.when(y < 2)
        def _():
            send_m2(g).wait_recv()

        @pl.when((y >= 2) & low_h)
        def _():
            send_d2(g, ds.at[g, 0], 0, 0, 2).wait_recv()
            send_d2(g, ds.at[g, 0], 0, 1, 2).wait_recv()

        total = (
            own[g]
            + landed[g, pl.ds(0, ROWS), :].astype(F32)
            + landed[g, pl.ds(ROWS, ROWS), :].astype(F32)
        )
        kvo[g] = total.astype(BF16)
        return 0

    lax.fori_loop(0, 4, settle, 0)
    total = w_own[...]
    for k in range(3):
        wait_wh(k)
        total = total + wf[k].astype(F32)
    dw_ref[...] = total

    send_az_up().wait_send()
    send_az_down().wait_send()
    send_az_relay().wait_send()

    def drain(g, _):
        send_cot(g).wait_send()
        for d in range(1, 4):
            send_ay(g, d).wait_send()
            send_wy(g, d).wait_send()
            send_wl(g, d).wait_send()

        @pl.when(g != h)
        def _():
            send_wh(g).wait_send()

        @pl.when(y < 3)
        def _():
            send_n1(g).wait_send()

        @pl.when(y < 2)
        def _():
            send_n2(g).wait_send()

        @pl.when((y >= 2) & low_h)
        def _():
            send_x1(g, 0, 0).wait_send()

        @pl.when(low_h)
        def _():
            send_x2_staged(g, 0, 0).wait_send()

        @pl.when(y >= 1)
        def _():
            send_m1(g).wait_send()

        @pl.when(y >= 2)
        def _():
            send_m2(g).wait_send()

        @pl.when((y < 2) & high_h)
        def _():
            send_d1(g, 0, 0, 0, 0).wait_send()
            send_d1(g, 0, 0, 1, 0).wait_send()

        @pl.when((y == 0) & high_h)
        def _():
            send_d1(g, 0, 0, 2, 0).wait_send()
            send_fwd(g).wait_send()

        @pl.when(high_h)
        def _():
            send_d2(g, ds.at[g, 0], 0, 0, 2).wait_send()

        return 0

    lax.fori_loop(0, 4, drain, 0)


def finish(dq_ref, dkv_ref, da_ref, dw_ref, dq_hbm, dkv_hbm, da_hbm, dw_hbm, sems):
    copies = [
        (dq_ref.at[g], dq_hbm.at[0, 0, :, pl.ds(g * WIDE, WIDE)]) for g in range(4)
    ] + [
        (dkv_ref.at[g], dkv_hbm.at[0, 0, :, pl.ds(g * PAIR, PAIR)]) for g in range(4)
    ] + [(da_ref, da_hbm.at[0, 0]), (dw_ref, dw_hbm.at[0])]
    copies = [
        pltpu.make_async_copy(src, dst, sems.at[k]) for k, (src, dst) in enumerate(copies)
    ]
    for copy in copies:
        copy.start()
    for copy in copies:
        copy.wait()


def per_device(frozen_queries, key_value_pairs, adapter_input, adapter_up_matrix, upstream, document_index):
    hbm = pl.BlockSpec(memory_space=pltpu.HBM)
    vmem = pl.BlockSpec(memory_space=pltpu.VMEM)
    dma = pltpu.SemaphoreType.DMA
    scratch = [
        pltpu.VMEM((4, ROWS, WIDE), BF16),
        pltpu.VMEM((4, ROWS, WIDE), BF16),
        pltpu.VMEM((4, 3 * ROWS, PAIR), BF16),
        pltpu.VMEM((4, HALF, PAIR), BF16),
        pltpu.VMEM((16, RANK, 256), BF16),
        pltpu.VMEM((RANK, ROWS), BF16),
        pltpu.VMEM((3 * ROWS, ROWS), F32),
        pltpu.VMEM((4, ROWS, PAIR), F32),
        pltpu.VMEM((4, 2 * ROWS, PAIR), BF16),
        pltpu.VMEM((4, 2 * ROWS, PAIR), BF16),
        pltpu.VMEM((4, 2, HALF, PAIR), BF16),
        pltpu.VMEM((4, HALF, PAIR), BF16),
        pltpu.VMEM((RANK, ROWS), F32),
        pltpu.VMEM((4, 4, RANK, 256), BF16),
        pltpu.VMEM((4, 3, RANK, 256), BF16),
        pltpu.VMEM((4, RANK, 256), BF16),
        pltpu.VMEM((4, 3, PART, 256), BF16),
        pltpu.VMEM((4, PART, 256), BF16),
        pltpu.VMEM((3, PART, 256), BF16),
        pltpu.VMEM((PART, 256), F32),
        dma((4,)), dma((4,)), dma, dma,
        dma((4,)), dma((4,)), dma((3,)), dma((3,)), dma((4, 3)), dma((4, 3)),
        dma((4,)), dma((4,)), dma((4,)), dma((4,)), dma((4,)),
        dma((4,)), dma((4,)), dma((4,)), dma((4, 4)),
        dma((4,)), dma((4,)), dma((4,)), dma((4,)),
        dma((4, 3)), dma((4, 2)), dma((4,)), dma((4, 2)),
        dma((4, 3)), dma((4, 3)), dma((4, 3)), dma((4, 3)), dma((4,)), dma((3,)),
    ]
    results = pl.pallas_call(
        kernel,
        out_shape=(
            jax.ShapeDtypeStruct((4, ROWS, WIDE), BF16),
            jax.ShapeDtypeStruct((4, ROWS, PAIR), BF16),
            jax.ShapeDtypeStruct((RANK, ROWS), BF16),
            jax.ShapeDtypeStruct((PART, 256), F32),
        ),
        in_specs=[hbm, hbm, hbm, hbm, hbm, vmem],
        out_specs=(vmem,) * 4,
        scratch_shapes=scratch,
        compiler_params=pltpu.CompilerParams(
            collective_id=0, has_side_effects=True, vmem_limit_bytes=62 << 20
        ),
    )(
        frozen_queries, key_value_pairs, jnp.swapaxes(adapter_input, 2, 3),
        adapter_up_matrix, upstream, document_index,
    )
    dq, dkv, da, dw = pl.pallas_call(
        finish,
        out_shape=(
            jax.ShapeDtypeStruct((1, 1, ROWS, 4 * WIDE), BF16),
            jax.ShapeDtypeStruct((1, 1, ROWS, 4 * PAIR), BF16),
            jax.ShapeDtypeStruct((1, 1, RANK, ROWS), BF16),
            jax.ShapeDtypeStruct((1, PART, 256), F32),
        ),
        in_specs=[vmem] * 4,
        out_specs=(hbm,) * 4,
        scratch_shapes=[dma((10,))],
        compiler_params=pltpu.CompilerParams(vmem_limit_bytes=62 << 20),
    )(*results)
    return dq, dkv, jnp.swapaxes(da, 2, 3), dw


def solution(mesh):
    placed = (
        P("section", "dp", "seq", None),
        P("section", "dp", "seq", None),
        P("section", "dp", "seq", None),
        P("section", None, "seq"),
        P("section", "dp", "seq", None),
        P("section", "dp", None),
    )
    return jax.shard_map(
        per_device,
        mesh=mesh,
        in_specs=placed,
        out_specs=(
            P("section", "dp", "seq", None),
            P("section", "dp", "seq", None),
            P("section", "dp", "seq", None),
            P("section", "dp", "seq"),
        ),
        check_vma=False,
    )
```

```python
import functools
import math

import jax
import jax.numpy as jnp
from jax import lax
from jax.experimental import pallas as pl
from jax.experimental.pallas import tpu as pltpu
from jax.sharding import PartitionSpec as P

HEAD = 128
ROWS = 128
HALF = ROWS // 2
PAIR = 2 * HEAD
WIDE = 8 * HEAD
RANK = 64
PART = RANK // 4
SCALE = 1.0 / math.sqrt(HEAD)
LOW = -1e30
MESH = pl.DeviceIdType.MESH
BF16 = jnp.bfloat16
F32 = jnp.float32


def dot(left, right, left_dim, right_dim):
    return lax.dot_general(
        left, right, (((left_dim,), (right_dim,)), ((), ())), preferred_element_type=F32
    )


def kernel(
    q_hbm, kv_hbm, a_hbm, w_hbm, up_hbm, doc_ref,
    dqv, kvo, da_ref, dw_ref,
    qf, cot, kvw, xs, wall, a_v, bias, own, dkvs, landed, ds, dso, da_acc,
    ws, wr, wz, wf,
    q_sem, kv_sem, a_sem, wl_sem,
    cot_s, cot_r, az_s, az_r, ay_s, ay_r,
    n1_s, n1_r, n2_s, n2_r, fw_s, x1_s, x1_r, x2_s, x2_r,
    m1_s, m1_r, m2_s, m2_r, d1_s, d1_r, d2_s, d2_r,
    wy_s, wy_r, wz_s, wz_r, far_sem,
):
    sec = lax.axis_index("section")
    p = lax.axis_index("seq")
    l = lax.axis_index("dp")
    y = lax.rem(p, 4)
    h = lax.div(p, 4)

    def mod4(v):
        return lax.rem(v + 8, 4)

    def at(h_, y_):
        return {"seq": h_ * 4 + y_}

    def remote(src, dst, s, r, where):
        return pltpu.make_async_remote_copy(
            src_ref=src, dst_ref=dst, send_sem=s, recv_sem=r,
            device_id=where, device_id_type=MESH,
        )

    def group(i, at_h=None):
        at_h = h if at_h is None else at_h
        zero = jnp.where(i < 2, i, 5 - i)
        two = i + 1 - 2 * lax.rem(i, 2)
        three = jnp.where(i == 0, 0, jnp.where(i == 1, 3, i - 1))
        return jnp.where(
            at_h == 0, zero, jnp.where(at_h == 1, i, jnp.where(at_h == 2, two, three))
        )

    def kv_cols(g):
        return pl.ds(pl.multiple_of(g * PAIR, PAIR), PAIR)

    def q_cols(g):
        return pl.ds(pl.multiple_of(g * WIDE, WIDE), WIDE)

    def load_q(g):
        return pltpu.make_async_copy(q_hbm.at[0, 0, :, q_cols(g)], qf.at[g], q_sem.at[g])

    def load_kv(g):
        return pltpu.make_async_copy(
            kv_hbm.at[0, 0, :, kv_cols(g)], kvw.at[g, pl.ds(2 * ROWS, ROWS)], kv_sem.at[g]
        )

    def load_a():
        return pltpu.make_async_copy(a_hbm.at[0, 0], a_v, a_sem)

    def load_w():
        return pltpu.make_async_copy(w_hbm.at[0], wall.at[p], wl_sem)

    def send_cot(g):
        return remote(
            up_hbm.at[0, 0, :, q_cols(g)], cot.at[g], cot_s.at[g], cot_r.at[g],
            {"section": lax.rem(sec + 7, 8)},
        )

    def send_az(away):
        src = wall.at[p]
        where = at(mod4(h - away), y)
        if isinstance(away, int) and away == 2:
            where["dp"] = mod4(l + 1)
        return remote(src, src, az_s.at[away - 1], az_r.at[away - 1], where)

    def wait_az(away):
        send_az(away).wait_recv()

    def send_ay(g, d):
        shard = wall.at[g * 4 + y]
        return remote(shard, shard, ay_s.at[g, d - 1], ay_r.at[g, d - 1], at(h, mod4(y + d)))

    def mine(g, first, rows):
        return kvw.at[g, pl.ds(2 * ROWS + first, rows)]

    def send_n1(g):
        return remote(
            mine(g, 0, ROWS), kvw.at[g, pl.ds(ROWS, ROWS)],
            n1_s.at[g], n1_r.at[g], at(h, mod4(y + 1)),
        )

    def send_n2(g):
        return remote(
            mine(g, 0, ROWS), kvw.at[g, pl.ds(0, ROWS)],
            n2_s.at[g], n2_r.at[g], at(h, mod4(y + 2)),
        )

    def send_fwd(g):
        return remote(
            kvw.at[g, pl.ds(ROWS, ROWS)], kvw.at[g, pl.ds(0, ROWS)],
            fw_s.at[g], n2_r.at[g], at(h, mod4(y + 1)),
        )

    def send_x1(g, first, where):
        return remote(
            mine(g, first, HALF), xs.at[g], x1_s.at[g], x1_r.at[g], at(h, where)
        )

    def send_x2_own(g, first, row, src_y):
        return remote(
            mine(g, first, HALF), kvw.at[g, pl.ds(row, HALF)],
            x2_s.at[g], x2_r.at[src_y, g], at(mod4(h + 1), 0),
        )

    def send_x2_staged(g, row, src_y):
        return remote(
            xs.at[g], kvw.at[g, pl.ds(row, HALF)], x2_s.at[g], x2_r.at[src_y, g],
            at(mod4(h + 1), 0),
        )

    def wait_x2(g, row, src_y):
        send_x2_staged(g, row, src_y).wait_recv()

    def send_m1(g):
        return remote(
            dkvs.at[g, pl.ds(ROWS, ROWS)], landed.at[g, pl.ds(0, ROWS)],
            m1_s.at[g], m1_r.at[g], at(h, mod4(y - 1)),
        )

    def send_m2(g):
        return remote(
            dkvs.at[g, pl.ds(0, ROWS)], landed.at[g, pl.ds(ROWS, ROWS)],
            m2_s.at[g], m2_r.at[g], at(h, mod4(y - 2)),
        )

    def send_d1(g, row, slot, k, where):
        return remote(
            dkvs.at[g, pl.ds(row, HALF)], ds.at[g, slot],
            d1_s.at[g, k], d1_r.at[g, slot], at(h, where),
        )

    def send_d2(g, src, row, k, where):
        return remote(
            src, landed.at[g, pl.ds(row, HALF)],
            d2_s.at[g], d2_r.at[g, k], at(mod4(h - 1), where),
        )

    def send_wy(g, d):
        to = mod4(y + d)
        return remote(ws.at[g, to], wr.at[g, d - 1], wy_s.at[g, d - 1], wy_r.at[g, d - 1], at(h, to))

    def send_wz(g, d):
        to = mod4(l + d)
        slot = mod4(h - g) * 4 + mod4(-d)
        where = at(g, y)
        where["dp"] = to
        return remote(
            wz.at[g, pl.ds(pl.multiple_of(to * PART, PART), PART)], wf.at[slot],
            wz_s.at[g, d], wz_r.at[slot], where,
        )

    def wait_wz(slot):
        remote(wf.at[0], wf.at[slot], wz_s.at[0, 0], wz_r.at[slot], at(mod4(h + 1), y)).wait_recv()

    low_h = h < 3
    early = (h == 0) | (h == 3)
    late = (h == 1) | (h == 2)
    high_h = h > 0

    load_w().start()
    for g in range(4):
        load_kv(g).start()
    load_a().start()
    for g in range(4):
        load_q(g).start()

    bar = pltpu.get_barrier_semaphore()

    def greet(where):
        pl.semaphore_signal(bar, inc=1, device_id=where, device_id_type=MESH)

    greet({"section": lax.rem(sec + 7, 8)})
    greet({"section": lax.rem(sec + 1, 8)})
    greet(at(mod4(h + 1), y))
    greet(at(mod4(h - 1), y))

    @pl.when(early)
    def _():
        greet({"seq": mod4(h + 2) * 4 + y, "dp": mod4(l - 1)})
        greet({"seq": mod4(h + 2) * 4 + y, "dp": mod4(l + 1)})

    for d in range(1, 4):
        greet(at(h, mod4(y + d)))
        greet({"dp": mod4(l + d)})

    @pl.when((y == 0) & high_h)
    def _():
        for k in range(1, 4):
            greet(at(h - 1, k))

    @pl.when((y >= 1) & low_h)
    def _():
        greet(at(h + 1, 0))

    @pl.when((y == 1) & high_h)
    def _():
        greet(at(h - 1, 2))

    @pl.when((y == 2) & low_h)
    def _():
        greet(at(h + 1, 1))

    extra = (
        jnp.where((y == 0) & high_h, 3, 0)
        + jnp.where((y >= 1) & low_h, 1, 0)
        + jnp.where((y == 1) & high_h, 1, 0)
        + jnp.where((y == 2) & low_h, 1, 0)
        + jnp.where(late, 2, 0)
    )
    pl.semaphore_wait(bar, 10 + extra)

    @pl.when(late)
    def _():
        pl.semaphore_signal(
            far_sem, inc=1, device_id={"seq": mod4(h + 2) * 4 + y, "dp": mod4(l - 1)},
            device_id_type=MESH,
        )


    for g in range(4):
        load_kv(g).wait()

    @pl.when((y == 2) & low_h)
    def _():
        for j in range(4):
            send_x1(group(j, h + 1), HALF, 1).start()

    @pl.when((y == 3) & low_h)
    def _():
        for j in range(4):
            send_x1(group(j, h + 1), 0, 0).start()

    load_w().wait()
    send_az(1).start()

    @pl.when(late)
    def _():
        send_az(2).start()

    send_az(3).start()
    for d in (1, 3, 2):
        send_ay(h, d).start()

    @pl.when((y == 2) & low_h)
    def _():
        for j in range(4):
            send_x2_own(group(j, h + 1), 0, 0, 2).start()

    @pl.when((y == 3) & low_h)
    def _():
        for j in range(4):
            send_x2_own(group(j, h + 1), HALF, 192, 3).start()

    send_cot(group(0)).start()

    for i in range(4):
        g = group(i)
        if i > 0:
            send_cot(g).start()

        @pl.when(y < 3)
        def _():
            send_n1(g).start()

        @pl.when(y < 2)
        def _():
            send_n2(g).start()

    def docs(block):
        return doc_ref[0, :, pl.ds(pl.multiple_of(block * ROWS, ROWS), ROWS)].astype(F32)

    my_docs = jnp.broadcast_to(docs(p), (ROWS, ROWS))
    key_row = lax.broadcasted_iota(jnp.int32, (ROWS, ROWS), 0)
    query_col = lax.broadcasted_iota(jnp.int32, (ROWS, ROWS), 1)
    for k in range(3):
        back = 2 - k
        block = jnp.maximum(p - back, 0)
        theirs = jnp.broadcast_to(docs(block), (ROWS, ROWS)).T
        seen = theirs == my_docs
        if back == 0:
            seen = seen & (key_row <= query_col)
        else:
            seen = seen & (jnp.broadcast_to(p, (ROWS, ROWS)) >= back)
        bias[pl.ds(k * ROWS, ROWS), :] = jnp.where(seen, 0.0, LOW)

    @pl.when(p < 2)
    def _():
        kvw[:, pl.ds(0, ROWS), :] = jnp.zeros((4, ROWS, PAIR), BF16)

    @pl.when(p < 1)
    def _():
        kvw[:, pl.ds(ROWS, ROWS), :] = jnp.zeros((4, ROWS, PAIR), BF16)

    @pl.when((y == 3) | (p == 14))
    def _():
        landed[:, pl.ds(ROWS, ROWS), :] = jnp.zeros((4, ROWS, PAIR), BF16)

    @pl.when(p == 15)
    def _():
        landed[:, pl.ds(0, ROWS), :] = jnp.zeros((4, ROWS, PAIR), BF16)

    da_acc[...] = jnp.zeros((RANK, ROWS), F32)

    @pl.when((y == 1) & low_h)
    def _():
        for j in range(4):
            g = group(j, h + 1)
            send_x1(g, HALF, 1).wait_recv()
            send_x2_staged(g, 64, 1).start()

    @pl.when((y == 0) & low_h)
    def _():
        for j in range(4):
            g = group(j, h + 1)
            send_x1(g, 0, 0).wait_recv()
            send_x2_staged(g, 128, 0).start()

    @pl.when(early)
    def _():
        pl.semaphore_wait(far_sem, 1)
        send_az(2).start()

    def pass_shard(g):
        away = mod4(g - h)

        @pl.when(away > 0)
        def _():
            wait_az(away)

            for d in (1, 3, 2):
                send_ay(g, d).start()

    pass_shard(group(0))
    load_a().wait()

    def work(r):
        i = group(r)
        g = i
        load_q(i).wait()

        @pl.when((y == 0) & high_h)
        def _():
            wait_x2(i, 128, 0)
            wait_x2(i, 192, 3)
            send_fwd(i).start()
            wait_x2(i, 64, 1)
            wait_x2(i, 0, 2)

        @pl.when(y >= 1)
        def _():
            send_n1(i).wait_recv()

        @pl.when((y >= 2) | ((y == 1) & high_h))
        def _():
            send_n2(i).wait_recv()

        send_cot(i).wait_recv()

        @pl.when(r < 3)
        def _():
            pass_shard(group(jnp.minimum(r + 1, 3)))

        for d in (1, 3, 2):
            send_ay(i, d).wait_recv()

        a_cols = a_v[...]
        w_g = jnp.concatenate([wall[g * 4 + k] for k in range(4)], axis=1)
        keys = kvw[i, :, :HEAD]
        values = kvw[i, :, HEAD:]
        seen = jnp.concatenate([bias[...]] * 8, axis=1)
        queries = (qf[i].astype(F32) + dot(a_cols, w_g, 0, 0)).astype(BF16)
        cots = cot[i]
        q_rows = jnp.concatenate([queries[:, k * HEAD:(k + 1) * HEAD] for k in range(8)], axis=0)
        c_rows = jnp.concatenate([cots[:, k * HEAD:(k + 1) * HEAD] for k in range(8)], axis=0)
        scores = dot(keys, q_rows, 1, 1) * (SCALE * math.log2(math.e)) + seen
        top = jnp.max(scores, axis=0, keepdims=True)
        raised = jnp.exp2(scores - top)
        probs = raised * (1.0 / jnp.sum(raised, axis=0, keepdims=True))
        dprobs = dot(values, c_rows, 1, 1)
        deltas = jnp.sum(probs * dprobs, axis=0, keepdims=True)
        dscores = (probs * (dprobs - deltas)).astype(BF16)
        d_value = dot(probs.astype(BF16), c_rows, 1, 0)
        d_key = dot(dscores, q_rows, 1, 0)
        grads = jnp.concatenate([d_key * SCALE, d_value], axis=1)
        own[i] = grads[2 * ROWS:]
        dkvs[i] = grads[:2 * ROWS].astype(BF16)

        @pl.when((y == 0) & high_h)
        def _():
            send_d1(i, 64, 0, 1, 1).start()
            send_d1(i, 192, 0, 2, 3).start()
            send_d1(i, 0, 0, 0, 2).start()

        @pl.when((y == 1) & high_h)
        def _():
            send_d1(i, 64, 1, 1, 3).start()
            send_d1(i, 0, 0, 0, 0).start()

        @pl.when(y >= 1)
        def _():
            send_m1(i).start()

        @pl.when(y >= 2)
        def _():
            send_m2(i).start()

        dq_rows = (dot(dscores, keys, 0, 0) * SCALE).astype(BF16)
        dq = jnp.concatenate([dq_rows[k * ROWS:(k + 1) * ROWS] for k in range(8)], axis=1)
        dqv[i] = dq
        dw = dot(a_cols, dq, 1, 0).astype(BF16)
        for k in range(4):
            ws[i, k] = dw[:, k * 256:(k + 1) * 256]
        for d in (1, 3, 2):
            send_wy(i, d).start()
        da_acc[...] += dot(w_g, dq, 1, 1)

    def second(r):
        i = group(r)

        @pl.when((y == 0) & high_h)
        def _():
            send_d1(i, 0, 0, 0, 0).wait_recv()
            dso[i] = (ds[i, 0].astype(F32) + dkvs[i, pl.ds(ROWS, HALF), :].astype(F32)).astype(BF16)
            send_d2(i, dso.at[i], 0, 0, 3).start()

        @pl.when((y == 3) & high_h)
        def _():
            send_d1(i, 0, 0, 0, 0).wait_recv()
            send_d1(i, 0, 1, 0, 0).wait_recv()
            dso[i] = (ds[i, 0].astype(F32) + ds[i, 1].astype(F32)).astype(BF16)
            send_d2(i, dso.at[i], 64, 1, 3).start()

        @pl.when((y == 1) & high_h)
        def _():
            send_d1(i, 0, 0, 0, 0).wait_recv()
            send_d2(i, ds.at[i, 0], 192, 1, 2).start()

        @pl.when((y == 2) & high_h)
        def _():
            send_d1(i, 0, 0, 0, 0).wait_recv()
            send_d2(i, ds.at[i, 0], 128, 0, 2).start()

        total = ws[i, y].astype(F32)
        for d in range(1, 4):
            send_wy(i, d).wait_recv()
            total = total + wr[i, d - 1].astype(F32)
        wz[i] = total.astype(BF16)
        for d in (1, 3, 2):
            send_wz(i, d).start()

        @pl.when(i != h)
        def _():
            send_wz(i, 0).start()

    def round_(r, _):
        @pl.when(r < 4)
        def _():
            work(r)

        @pl.when(r >= 1)
        def _():
            second(r - 1)

        return 0

    lax.fori_loop(0, 5, round_, 0)

    da_ref[...] = da_acc[...].astype(BF16)

    def settle(r, _):
        g = group(r)

        @pl.when(y < 3)
        def _():
            send_m1(g).wait_recv()

        @pl.when(y < 2)
        def _():
            send_m2(g).wait_recv()

        @pl.when((y >= 2) & low_h)
        def _():
            send_d2(g, ds.at[g, 0], 0, 0, 2).wait_recv()
            send_d2(g, ds.at[g, 0], 0, 1, 2).wait_recv()

        total = (
            own[g]
            + landed[g, pl.ds(0, ROWS), :].astype(F32)
            + landed[g, pl.ds(ROWS, ROWS), :].astype(F32)
        )
        kvo[g] = total.astype(BF16)
        return 0

    lax.fori_loop(0, 4, settle, 0)
    total = wz[h, pl.ds(pl.multiple_of(l * PART, PART), PART), :].astype(F32)
    for k in range(1, 16):
        wait_wz(k)
        total = total + wf[k].astype(F32)
    dw_ref[...] = total

    for away in range(1, 4):
        send_az(away).wait_send()

    def drain(g, _):
        send_cot(g).wait_send()
        for d in range(1, 4):
            send_ay(g, d).wait_send()
            send_wy(g, d).wait_send()
            send_wz(g, d).wait_send()

        @pl.when(g != h)
        def _():
            send_wz(g, 0).wait_send()

        @pl.when(y < 3)
        def _():
            send_n1(g).wait_send()

        @pl.when(y < 2)
        def _():
            send_n2(g).wait_send()

        @pl.when((y >= 2) & low_h)
        def _():
            send_x1(g, 0, 0).wait_send()

        @pl.when(low_h)
        def _():
            send_x2_staged(g, 0, 0).wait_send()

        @pl.when(y >= 1)
        def _():
            send_m1(g).wait_send()

        @pl.when(y >= 2)
        def _():
            send_m2(g).wait_send()

        @pl.when((y < 2) & high_h)
        def _():
            send_d1(g, 0, 0, 0, 0).wait_send()
            send_d1(g, 0, 0, 1, 0).wait_send()

        @pl.when((y == 0) & high_h)
        def _():
            send_d1(g, 0, 0, 2, 0).wait_send()
            send_fwd(g).wait_send()

        @pl.when(high_h)
        def _():
            send_d2(g, ds.at[g, 0], 0, 0, 2).wait_send()

        return 0

    lax.fori_loop(0, 4, drain, 0)


def finish(dq_ref, dkv_ref, da_ref, dw_ref, dq_hbm, dkv_hbm, da_hbm, dw_hbm, sems):
    copies = [
        (dq_ref.at[g], dq_hbm.at[0, 0, :, pl.ds(g * WIDE, WIDE)]) for g in range(4)
    ] + [
        (dkv_ref.at[g], dkv_hbm.at[0, 0, :, pl.ds(g * PAIR, PAIR)]) for g in range(4)
    ] + [(da_ref, da_hbm.at[0, 0]), (dw_ref, dw_hbm.at[0])]
    copies = [
        pltpu.make_async_copy(src, dst, sems.at[k]) for k, (src, dst) in enumerate(copies)
    ]
    for copy in copies:
        copy.start()
    for copy in copies:
        copy.wait()


def per_device(frozen_queries, key_value_pairs, adapter_input, adapter_up_matrix, upstream, document_index):
    hbm = pl.BlockSpec(memory_space=pltpu.HBM)
    vmem = pl.BlockSpec(memory_space=pltpu.VMEM)
    dma = pltpu.SemaphoreType.DMA
    scratch = [
        pltpu.VMEM((4, ROWS, WIDE), BF16),
        pltpu.VMEM((4, ROWS, WIDE), BF16),
        pltpu.VMEM((4, 3 * ROWS, PAIR), BF16),
        pltpu.VMEM((4, HALF, PAIR), BF16),
        pltpu.VMEM((16, RANK, 256), BF16),
        pltpu.VMEM((RANK, ROWS), BF16),
        pltpu.VMEM((3 * ROWS, ROWS), F32),
        pltpu.VMEM((4, ROWS, PAIR), F32),
        pltpu.VMEM((4, 2 * ROWS, PAIR), BF16),
        pltpu.VMEM((4, 2 * ROWS, PAIR), BF16),
        pltpu.VMEM((4, 2, HALF, PAIR), BF16),
        pltpu.VMEM((4, HALF, PAIR), BF16),
        pltpu.VMEM((RANK, ROWS), F32),
        pltpu.VMEM((4, 4, RANK, 256), BF16),
        pltpu.VMEM((4, 3, RANK, 256), BF16),
        pltpu.VMEM((4, RANK, 256), BF16),
        pltpu.VMEM((16, PART, 256), BF16),
        dma((4,)), dma((4,)), dma, dma,
        dma((4,)), dma((4,)), dma((3,)), dma((3,)), dma((4, 3)), dma((4, 3)),
        dma((4,)), dma((4,)), dma((4,)), dma((4,)), dma((4,)),
        dma((4,)), dma((4,)), dma((4,)), dma((4, 4)),
        dma((4,)), dma((4,)), dma((4,)), dma((4,)),
        dma((4, 3)), dma((4, 2)), dma((4,)), dma((4, 2)),
        dma((4, 3)), dma((4, 3)), dma((4, 4)), dma((16,)), pltpu.SemaphoreType.REGULAR,
    ]
    results = pl.pallas_call(
        kernel,
        out_shape=(
            jax.ShapeDtypeStruct((4, ROWS, WIDE), BF16),
            jax.ShapeDtypeStruct((4, ROWS, PAIR), BF16),
            jax.ShapeDtypeStruct((RANK, ROWS), BF16),
            jax.ShapeDtypeStruct((PART, 256), F32),
        ),
        in_specs=[hbm, hbm, hbm, hbm, hbm, vmem],
        out_specs=(vmem,) * 4,
        scratch_shapes=scratch,
        compiler_params=pltpu.CompilerParams(
            collective_id=0, has_side_effects=True, vmem_limit_bytes=54 << 20
        ),
    )(
        frozen_queries, key_value_pairs, jnp.swapaxes(adapter_input, 2, 3),
        adapter_up_matrix, upstream, document_index,
    )
    dq, dkv, da, dw = pl.pallas_call(
        finish,
        out_shape=(
            jax.ShapeDtypeStruct((1, 1, ROWS, 4 * WIDE), BF16),
            jax.ShapeDtypeStruct((1, 1, ROWS, 4 * PAIR), BF16),
            jax.ShapeDtypeStruct((1, 1, RANK, ROWS), BF16),
            jax.ShapeDtypeStruct((1, PART, 256), F32),
        ),
        in_specs=[vmem] * 4,
        out_specs=(hbm,) * 4,
        scratch_shapes=[dma((10,))],
        compiler_params=pltpu.CompilerParams(vmem_limit_bytes=54 << 20),
    )(*results)
    return dq, dkv, jnp.swapaxes(da, 2, 3), dw


def solution(mesh):
    placed = (
        P("section", "dp", "seq", None),
        P("section", "dp", "seq", None),
        P("section", "dp", "seq", None),
        P("section", None, "seq"),
        P("section", "dp", "seq", None),
        P("section", "dp", None),
    )
    return jax.shard_map(
        per_device,
        mesh=mesh,
        in_specs=placed,
        out_specs=(
            P("section", "dp", "seq", None),
            P("section", "dp", "seq", None),
            P("section", "dp", "seq", None),
            P("section", "dp", "seq"),
        ),
        check_vma=False,
    )
```

```python
import functools
import math

import jax
import jax.numpy as jnp
from jax import lax
from jax.experimental import pallas as pl
from jax.experimental.pallas import tpu as pltpu
from jax.sharding import PartitionSpec as P

HEAD = 128
ROWS = 128
HALF = ROWS // 2
PAIR = 2 * HEAD
WIDE = 8 * HEAD
RANK = 64
PART = RANK // 4
SCALE = 1.0 / math.sqrt(HEAD)
LOW = -1e30
MESH = pl.DeviceIdType.MESH
BF16 = jnp.bfloat16
F32 = jnp.float32


def dot(left, right, left_dim, right_dim):
    return lax.dot_general(
        left, right, (((left_dim,), (right_dim,)), ((), ())), preferred_element_type=F32
    )


def kernel(
    q_hbm, kv_hbm, a_hbm, w_hbm, up_hbm, doc_ref,
    dqv, kvo, da_ref, dw_ref,
    qf, cot, kvw, xs, wall, a_v, bias, own, dkvs, landed, ds, dso, da_acc,
    ws, wr, wz, wf,
    q_sem, kv_sem, a_sem, wl_sem,
    cot_s, cot_r, az_s, az_r, ay_s, ay_r,
    n1_s, n1_r, n2_s, n2_r, fw_s, x1_s, x1_r, x2_s, x2_r,
    m1_s, m1_r, m2_s, m2_r, d1_s, d1_r, d2_s, d2_r,
    wy_s, wy_r, wz_s, wz_r, far_sem,
):
    sec = lax.axis_index("section")
    p = lax.axis_index("seq")
    l = lax.axis_index("dp")
    y = lax.rem(p, 4)
    h = lax.div(p, 4)

    def mod4(v):
        return lax.rem(v + 8, 4)

    def at(h_, y_):
        return {"seq": h_ * 4 + y_}

    def remote(src, dst, s, r, where):
        return pltpu.make_async_remote_copy(
            src_ref=src, dst_ref=dst, send_sem=s, recv_sem=r,
            device_id=where, device_id_type=MESH,
        )

    def group(i, at_h=None):
        at_h = h if at_h is None else at_h
        zero = jnp.where(i < 2, i, 5 - i)
        two = i + 1 - 2 * lax.rem(i, 2)
        three = jnp.where(i == 0, 0, jnp.where(i == 1, 3, i - 1))
        return jnp.where(
            at_h == 0, zero, jnp.where(at_h == 1, i, jnp.where(at_h == 2, two, three))
        )

    def kv_cols(g):
        return pl.ds(pl.multiple_of(g * PAIR, PAIR), PAIR)

    def q_cols(g):
        return pl.ds(pl.multiple_of(g * WIDE, WIDE), WIDE)

    def load_q(g):
        return pltpu.make_async_copy(q_hbm.at[0, 0, :, q_cols(g)], qf.at[g], q_sem.at[g])

    def load_kv(g):
        return pltpu.make_async_copy(
            kv_hbm.at[0, 0, :, kv_cols(g)], kvw.at[g, pl.ds(2 * ROWS, ROWS)], kv_sem.at[g]
        )

    def load_a():
        return pltpu.make_async_copy(a_hbm.at[0, 0], a_v, a_sem)

    def load_w():
        return pltpu.make_async_copy(w_hbm.at[0], wall.at[p], wl_sem)

    def send_cot(g):
        return remote(
            up_hbm.at[0, 0, :, q_cols(g)], cot.at[g], cot_s.at[g], cot_r.at[g],
            {"section": lax.rem(sec + 7, 8)},
        )

    def send_az(away):
        src = wall.at[p]
        where = at(mod4(h - away), y)
        if isinstance(away, int) and away == 2:
            where["dp"] = mod4(l + 1)
        return remote(src, src, az_s.at[away - 1], az_r.at[away - 1], where)

    def wait_az(away):
        send_az(away).wait_recv()

    def send_ay(g, d):
        shard = wall.at[g * 4 + y]
        return remote(shard, shard, ay_s.at[g, d - 1], ay_r.at[g, d - 1], at(h, mod4(y + d)))

    def mine(g, first, rows):
        return kvw.at[g, pl.ds(2 * ROWS + first, rows)]

    def send_n1(g):
        return remote(
            mine(g, 0, ROWS), kvw.at[g, pl.ds(ROWS, ROWS)],
            n1_s.at[g], n1_r.at[g], at(h, mod4(y + 1)),
        )

    def send_n2(g):
        return remote(
            mine(g, 0, ROWS), kvw.at[g, pl.ds(0, ROWS)],
            n2_s.at[g], n2_r.at[g], at(h, mod4(y + 2)),
        )

    def send_fwd(g):
        return remote(
            kvw.at[g, pl.ds(ROWS, ROWS)], kvw.at[g, pl.ds(0, ROWS)],
            fw_s.at[g], n2_r.at[g], at(h, mod4(y + 1)),
        )

    def send_x1(g, first, where):
        return remote(
            mine(g, first, HALF), xs.at[g], x1_s.at[g], x1_r.at[g], at(h, where)
        )

    def send_x2_own(g, first, row, src_y):
        return remote(
            mine(g, first, HALF), kvw.at[g, pl.ds(row, HALF)],
            x2_s.at[g], x2_r.at[src_y, g], at(mod4(h + 1), 0),
        )

    def send_x2_staged(g, row, src_y):
        return remote(
            xs.at[g], kvw.at[g, pl.ds(row, HALF)], x2_s.at[g], x2_r.at[src_y, g],
            at(mod4(h + 1), 0),
        )

    def wait_x2(g, row, src_y):
        send_x2_staged(g, row, src_y).wait_recv()

    def send_m1(g):
        return remote(
            dkvs.at[g, pl.ds(ROWS, ROWS)], landed.at[g, pl.ds(0, ROWS)],
            m1_s.at[g], m1_r.at[g], at(h, mod4(y - 1)),
        )

    def send_m2(g):
        return remote(
            dkvs.at[g, pl.ds(0, ROWS)], landed.at[g, pl.ds(ROWS, ROWS)],
            m2_s.at[g], m2_r.at[g], at(h, mod4(y - 2)),
        )

    def send_d1(g, row, slot, k, where):
        return remote(
            dkvs.at[g, pl.ds(row, HALF)], ds.at[g, slot],
            d1_s.at[g, k], d1_r.at[g, slot], at(h, where),
        )

    def send_d2(g, src, row, k, where):
        return remote(
            src, landed.at[g, pl.ds(row, HALF)],
            d2_s.at[g], d2_r.at[g, k], at(mod4(h - 1), where),
        )

    def send_wy(g, d):
        to = mod4(y + d)
        return remote(ws.at[g, to], wr.at[g, d - 1], wy_s.at[g, d - 1], wy_r.at[g, d - 1], at(h, to))

    def send_wz(g, d):
        to = mod4(l + d)
        slot = mod4(h - g) * 4 + mod4(-d)
        where = at(g, y)
        where["dp"] = to
        return remote(
            wz.at[g, pl.ds(pl.multiple_of(to * PART, PART), PART)], wf.at[slot],
            wz_s.at[g, d], wz_r.at[slot], where,
        )

    def wait_wz(slot):
        remote(wf.at[0], wf.at[slot], wz_s.at[0, 0], wz_r.at[slot], at(mod4(h + 1), y)).wait_recv()

    low_h = h < 3
    early = (h == 0) | (h == 3)
    late = (h == 1) | (h == 2)
    high_h = h > 0

    load_w().start()
    for g in range(4):
        load_kv(g).start()
    load_a().start()
    for g in range(4):
        load_q(g).start()

    bar = pltpu.get_barrier_semaphore()

    def greet(where):
        pl.semaphore_signal(bar, inc=1, device_id=where, device_id_type=MESH)

    greet({"section": lax.rem(sec + 7, 8)})
    greet({"section": lax.rem(sec + 1, 8)})
    greet(at(mod4(h + 1), y))
    greet(at(mod4(h - 1), y))

    @pl.when(early)
    def _():
        greet({"seq": mod4(h + 2) * 4 + y, "dp": mod4(l - 1)})
        greet({"seq": mod4(h + 2) * 4 + y, "dp": mod4(l + 1)})

    for d in range(1, 4):
        greet(at(h, mod4(y + d)))
        greet({"dp": mod4(l + d)})

    @pl.when((y == 0) & high_h)
    def _():
        for k in range(1, 4):
            greet(at(h - 1, k))

    @pl.when((y >= 1) & low_h)
    def _():
        greet(at(h + 1, 0))

    @pl.when((y == 1) & high_h)
    def _():
        greet(at(h - 1, 2))

    @pl.when((y == 2) & low_h)
    def _():
        greet(at(h + 1, 1))

    extra = (
        jnp.where((y == 0) & high_h, 3, 0)
        + jnp.where((y >= 1) & low_h, 1, 0)
        + jnp.where((y == 1) & high_h, 1, 0)
        + jnp.where((y == 2) & low_h, 1, 0)
        + jnp.where(late, 2, 0)
    )
    pl.semaphore_wait(bar, 10 + extra)

    @pl.when(late)
    def _():
        pl.semaphore_signal(
            far_sem, inc=1, device_id={"seq": mod4(h + 2) * 4 + y, "dp": mod4(l - 1)},
            device_id_type=MESH,
        )


    for g in range(4):
        load_kv(g).wait()

    @pl.when((y == 2) & low_h)
    def _():
        for j in range(4):
            send_x1(group(j, h + 1), HALF, 1).start()

    @pl.when((y == 3) & low_h)
    def _():
        for j in range(4):
            send_x1(group(j, h + 1), 0, 0).start()

    load_w().wait()
    send_az(1).start()

    @pl.when(late)
    def _():
        send_az(2).start()

    send_az(3).start()
    for d in (1, 3, 2):
        send_ay(h, d).start()

    @pl.when((y == 2) & low_h)
    def _():
        for j in range(4):
            send_x2_own(group(j, h + 1), 0, 0, 2).start()

    @pl.when((y == 3) & low_h)
    def _():
        for j in range(4):
            send_x2_own(group(j, h + 1), HALF, 192, 3).start()

    send_cot(group(0)).start()

    for i in range(4):
        g = group(i)
        if i > 0:
            send_cot(g).start()

        @pl.when(y < 3)
        def _():
            send_n1(g).start()

        @pl.when(y < 2)
        def _():
            send_n2(g).start()

    def docs(block):
        return doc_ref[0, :, pl.ds(pl.multiple_of(block * ROWS, ROWS), ROWS)].astype(F32)

    my_docs = jnp.broadcast_to(docs(p), (ROWS, ROWS))
    key_row = lax.broadcasted_iota(jnp.int32, (ROWS, ROWS), 0)
    query_col = lax.broadcasted_iota(jnp.int32, (ROWS, ROWS), 1)
    for k in range(3):
        back = 2 - k
        block = jnp.maximum(p - back, 0)
        theirs = jnp.broadcast_to(docs(block), (ROWS, ROWS)).T
        seen = theirs == my_docs
        if back == 0:
            seen = seen & (key_row <= query_col)
        else:
            seen = seen & (jnp.broadcast_to(p, (ROWS, ROWS)) >= back)
        bias[pl.ds(k * ROWS, ROWS), :] = jnp.where(seen, 0.0, LOW)

    @pl.when(p < 2)
    def _():
        kvw[:, pl.ds(0, ROWS), :] = jnp.zeros((4, ROWS, PAIR), BF16)

    @pl.when(p < 1)
    def _():
        kvw[:, pl.ds(ROWS, ROWS), :] = jnp.zeros((4, ROWS, PAIR), BF16)

    @pl.when((y == 3) | (p == 14))
    def _():
        landed[:, pl.ds(ROWS, ROWS), :] = jnp.zeros((4, ROWS, PAIR), BF16)

    @pl.when(p == 15)
    def _():
        landed[:, pl.ds(0, ROWS), :] = jnp.zeros((4, ROWS, PAIR), BF16)

    da_acc[...] = jnp.zeros((RANK, ROWS), F32)

    @pl.when((y == 1) & low_h)
    def _():
        for j in range(4):
            g = group(j, h + 1)
            send_x1(g, HALF, 1).wait_recv()
            send_x2_staged(g, 64, 1).start()

    @pl.when((y == 0) & low_h)
    def _():
        for j in range(4):
            g = group(j, h + 1)
            send_x1(g, 0, 0).wait_recv()
            send_x2_staged(g, 128, 0).start()

    @pl.when(early)
    def _():
        pl.semaphore_wait(far_sem, 1)
        send_az(2).start()

    def pass_shard(g):
        away = mod4(g - h)

        @pl.when(away > 0)
        def _():
            wait_az(away)

            for d in (1, 3, 2):
                send_ay(g, d).start()

    pass_shard(group(0))
    load_a().wait()

    def work(r):
        i = group(r)
        g = i
        load_q(i).wait()

        @pl.when((y == 0) & high_h)
        def _():
            wait_x2(i, 128, 0)
            wait_x2(i, 192, 3)
            send_fwd(i).start()
            wait_x2(i, 64, 1)
            wait_x2(i, 0, 2)

        @pl.when(y >= 1)
        def _():
            send_n1(i).wait_recv()

        @pl.when((y >= 2) | ((y == 1) & high_h))
        def _():
            send_n2(i).wait_recv()

        send_cot(i).wait_recv()

        @pl.when(r < 3)
        def _():
            pass_shard(group(jnp.minimum(r + 1, 3)))

        for d in (1, 3, 2):
            send_ay(i, d).wait_recv()

        a_cols = a_v[...]
        w_g = jnp.concatenate([wall[g * 4 + k] for k in range(4)], axis=1)
        keys = kvw[i, :, :HEAD]
        values = kvw[i, :, HEAD:]
        seen = jnp.concatenate([bias[...]] * 8, axis=1)
        queries = (qf[i].astype(F32) + dot(a_cols, w_g, 0, 0)).astype(BF16)
        cots = cot[i]
        q_rows = jnp.concatenate([queries[:, k * HEAD:(k + 1) * HEAD] for k in range(8)], axis=0)
        c_rows = jnp.concatenate([cots[:, k * HEAD:(k + 1) * HEAD] for k in range(8)], axis=0)
        scores = dot(keys, q_rows, 1, 1) * (SCALE * math.log2(math.e)) + seen
        top = jnp.max(scores, axis=0, keepdims=True)
        raised = jnp.exp2(scores - top)
        probs = raised * (1.0 / jnp.sum(raised, axis=0, keepdims=True))
        dprobs = dot(values, c_rows, 1, 1)
        deltas = jnp.sum(probs * dprobs, axis=0, keepdims=True)
        dscores = (probs * (dprobs - deltas)).astype(BF16)
        d_value = dot(probs.astype(BF16), c_rows, 1, 0)
        d_key = dot(dscores, q_rows, 1, 0)
        grads = jnp.concatenate([d_key * SCALE, d_value], axis=1)
        own[i] = grads[2 * ROWS:]
        dkvs[i] = grads[:2 * ROWS].astype(BF16)

        @pl.when((y == 0) & high_h)
        def _():
            send_d1(i, 64, 0, 1, 1).start()
            send_d1(i, 192, 0, 2, 3).start()
            send_d1(i, 0, 0, 0, 2).start()

        @pl.when((y == 1) & high_h)
        def _():
            send_d1(i, 64, 1, 1, 3).start()
            send_d1(i, 0, 0, 0, 0).start()

        @pl.when(y >= 1)
        def _():
            send_m1(i).start()

        @pl.when(y >= 2)
        def _():
            send_m2(i).start()

        dq_rows = (dot(dscores, keys, 0, 0) * SCALE).astype(BF16)
        dq = jnp.concatenate([dq_rows[k * ROWS:(k + 1) * ROWS] for k in range(8)], axis=1)
        dqv[i] = dq
        dw = dot(a_cols, dq, 1, 0).astype(BF16)
        for k in range(4):
            ws[i, k] = dw[:, k * 256:(k + 1) * 256]
        for d in (1, 3, 2):
            send_wy(i, d).start()
        da_acc[...] += dot(w_g, dq, 1, 1)

    def second(r):
        i = group(r)

        @pl.when((y == 0) & high_h)
        def _():
            send_d1(i, 0, 0, 0, 0).wait_recv()
            dso[i] = (ds[i, 0].astype(F32) + dkvs[i, pl.ds(ROWS, HALF), :].astype(F32)).astype(BF16)
            send_d2(i, dso.at[i], 0, 0, 3).start()

        @pl.when((y == 3) & high_h)
        def _():
            send_d1(i, 0, 0, 0, 0).wait_recv()
            send_d1(i, 0, 1, 0, 0).wait_recv()
            dso[i] = (ds[i, 0].astype(F32) + ds[i, 1].astype(F32)).astype(BF16)
            send_d2(i, dso.at[i], 64, 1, 3).start()

        @pl.when((y == 1) & high_h)
        def _():
            send_d1(i, 0, 0, 0, 0).wait_recv()
            send_d2(i, ds.at[i, 0], 192, 1, 2).start()

        @pl.when((y == 2) & high_h)
        def _():
            send_d1(i, 0, 0, 0, 0).wait_recv()
            send_d2(i, ds.at[i, 0], 128, 0, 2).start()

        total = ws[i, y].astype(F32)
        for d in range(1, 4):
            send_wy(i, d).wait_recv()
            total = total + wr[i, d - 1].astype(F32)
        wz[i] = total.astype(BF16)
        for d in (1, 3, 2):
            send_wz(i, d).start()

        @pl.when(i != h)
        def _():
            send_wz(i, 0).start()

    def round_(r, _):
        @pl.when(r < 4)
        def _():
            work(r)

        @pl.when(r >= 1)
        def _():
            second(r - 1)

        return 0

    lax.fori_loop(0, 5, round_, 0)

    for away in range(1, 4):
        send_az(away).wait_send()

    def drain(g, _):
        send_cot(g).wait_send()
        for d in range(1, 4):
            send_ay(g, d).wait_send()
            send_wy(g, d).wait_send()

        @pl.when(y < 3)
        def _():
            send_n1(g).wait_send()

        @pl.when(y < 2)
        def _():
            send_n2(g).wait_send()

        @pl.when((y >= 2) & low_h)
        def _():
            send_x1(g, 0, 0).wait_send()

        @pl.when(low_h)
        def _():
            send_x2_staged(g, 0, 0).wait_send()

        @pl.when(y >= 1)
        def _():
            send_m1(g).wait_send()

        @pl.when(y >= 2)
        def _():
            send_m2(g).wait_send()

        @pl.when((y < 2) & high_h)
        def _():
            send_d1(g, 0, 0, 0, 0).wait_send()
            send_d1(g, 0, 0, 1, 0).wait_send()

        @pl.when((y == 0) & high_h)
        def _():
            send_d1(g, 0, 0, 2, 0).wait_send()
            send_fwd(g).wait_send()

        return 0

    lax.fori_loop(0, 4, drain, 0)

    da_ref[...] = da_acc[...].astype(BF16)

    def settle(r, _):
        g = group(r)

        @pl.when(y < 3)
        def _():
            send_m1(g).wait_recv()

        @pl.when(y < 2)
        def _():
            send_m2(g).wait_recv()

        @pl.when((y >= 2) & low_h)
        def _():
            send_d2(g, ds.at[g, 0], 0, 0, 2).wait_recv()
            send_d2(g, ds.at[g, 0], 0, 1, 2).wait_recv()

        total = (
            own[g]
            + landed[g, pl.ds(0, ROWS), :].astype(F32)
            + landed[g, pl.ds(ROWS, ROWS), :].astype(F32)
        )
        kvo[g] = total.astype(BF16)
        return 0

    lax.fori_loop(0, 4, settle, 0)
    total = wz[h, pl.ds(pl.multiple_of(l * PART, PART), PART), :].astype(F32)
    for k in range(1, 16):
        wait_wz(k)
        total = total + wf[k].astype(F32)
    dw_ref[...] = total

    def drain_last(g, _):
        for d in range(1, 4):
            send_wz(g, d).wait_send()

        @pl.when(g != h)
        def _():
            send_wz(g, 0).wait_send()

        @pl.when(high_h)
        def _():
            send_d2(g, ds.at[g, 0], 0, 0, 2).wait_send()

        return 0

    lax.fori_loop(0, 4, drain_last, 0)


def finish(dq_ref, dkv_ref, da_ref, dw_ref, dq_hbm, dkv_hbm, da_hbm, dw_hbm, sems):
    copies = [
        (dq_ref.at[g], dq_hbm.at[0, 0, :, pl.ds(g * WIDE, WIDE)]) for g in range(4)
    ] + [
        (dkv_ref.at[g], dkv_hbm.at[0, 0, :, pl.ds(g * PAIR, PAIR)]) for g in range(4)
    ] + [(da_ref, da_hbm.at[0, 0]), (dw_ref, dw_hbm.at[0])]
    copies = [
        pltpu.make_async_copy(src, dst, sems.at[k]) for k, (src, dst) in enumerate(copies)
    ]
    for copy in copies:
        copy.start()
    for copy in copies:
        copy.wait()


def per_device(frozen_queries, key_value_pairs, adapter_input, adapter_up_matrix, upstream, document_index):
    hbm = pl.BlockSpec(memory_space=pltpu.HBM)
    vmem = pl.BlockSpec(memory_space=pltpu.VMEM)
    dma = pltpu.SemaphoreType.DMA
    scratch = [
        pltpu.VMEM((4, ROWS, WIDE), BF16),
        pltpu.VMEM((4, ROWS, WIDE), BF16),
        pltpu.VMEM((4, 3 * ROWS, PAIR), BF16),
        pltpu.VMEM((4, HALF, PAIR), BF16),
        pltpu.VMEM((16, RANK, 256), BF16),
        pltpu.VMEM((RANK, ROWS), BF16),
        pltpu.VMEM((3 * ROWS, ROWS), F32),
        pltpu.VMEM((4, ROWS, PAIR), F32),
        pltpu.VMEM((4, 2 * ROWS, PAIR), BF16),
        pltpu.VMEM((4, 2 * ROWS, PAIR), BF16),
        pltpu.VMEM((4, 2, HALF, PAIR), BF16),
        pltpu.VMEM((4, HALF, PAIR), BF16),
        pltpu.VMEM((RANK, ROWS), F32),
        pltpu.VMEM((4, 4, RANK, 256), BF16),
        pltpu.VMEM((4, 3, RANK, 256), BF16),
        pltpu.VMEM((4, RANK, 256), BF16),
        pltpu.VMEM((16, PART, 256), BF16),
        dma((4,)), dma((4,)), dma, dma,
        dma((4,)), dma((4,)), dma((3,)), dma((3,)), dma((4, 3)), dma((4, 3)),
        dma((4,)), dma((4,)), dma((4,)), dma((4,)), dma((4,)),
        dma((4,)), dma((4,)), dma((4,)), dma((4, 4)),
        dma((4,)), dma((4,)), dma((4,)), dma((4,)),
        dma((4, 3)), dma((4, 2)), dma((4,)), dma((4, 2)),
        dma((4, 3)), dma((4, 3)), dma((4, 4)), dma((16,)), pltpu.SemaphoreType.REGULAR,
    ]
    results = pl.pallas_call(
        kernel,
        out_shape=(
            jax.ShapeDtypeStruct((4, ROWS, WIDE), BF16),
            jax.ShapeDtypeStruct((4, ROWS, PAIR), BF16),
            jax.ShapeDtypeStruct((RANK, ROWS), BF16),
            jax.ShapeDtypeStruct((PART, 256), F32),
        ),
        in_specs=[hbm, hbm, hbm, hbm, hbm, vmem],
        out_specs=(vmem,) * 4,
        scratch_shapes=scratch,
        compiler_params=pltpu.CompilerParams(
            collective_id=0, has_side_effects=True, vmem_limit_bytes=54 << 20
        ),
    )(
        frozen_queries, key_value_pairs, jnp.swapaxes(adapter_input, 2, 3),
        adapter_up_matrix, upstream, document_index,
    )
    dq, dkv, da, dw = pl.pallas_call(
        finish,
        out_shape=(
            jax.ShapeDtypeStruct((1, 1, ROWS, 4 * WIDE), BF16),
            jax.ShapeDtypeStruct((1, 1, ROWS, 4 * PAIR), BF16),
            jax.ShapeDtypeStruct((1, 1, RANK, ROWS), BF16),
            jax.ShapeDtypeStruct((1, PART, 256), F32),
        ),
        in_specs=[vmem] * 4,
        out_specs=(hbm,) * 4,
        scratch_shapes=[dma((10,))],
        compiler_params=pltpu.CompilerParams(vmem_limit_bytes=54 << 20),
    )(*results)
    return dq, dkv, jnp.swapaxes(da, 2, 3), dw


def solution(mesh):
    placed = (
        P("section", "dp", "seq", None),
        P("section", "dp", "seq", None),
        P("section", "dp", "seq", None),
        P("section", None, "seq"),
        P("section", "dp", "seq", None),
        P("section", "dp", None),
    )
    return jax.shard_map(
        per_device,
        mesh=mesh,
        in_specs=placed,
        out_specs=(
            P("section", "dp", "seq", None),
            P("section", "dp", "seq", None),
            P("section", "dp", "seq", None),
            P("section", "dp", "seq"),
        ),
        check_vma=False,
    )
```
